32 devices in a mesh: seq: 8 (over z, y), tp: 4 (over x, core).
Axes of the slice: x: 2, y: 2, z: 4, core: 2. Of those that a mesh axis runs over, the one named last changes fastest.
Arguments:
- layer_input: bfloat16 [1024, 1600], P(('seq', 'tp')), may hold values from -6 to 6
- out_grad: bfloat16 [1024, 1600], P(('seq', 'tp')), may hold values from -2.5 to 2.5
- w_in: bfloat16 [1600, 1600], P('tp'), may hold values from -0.15625 to 0.15625
- w_gate: bfloat16 [1600, 1600], P('tp'), may hold values from -0.15625 to 0.15625
- w_out: bfloat16 [1600, 1600], P('tp'), may hold values from -0.15625 to 0.15625
- b_proj: bfloat16 [16, 1024], P(None, 'seq'), may hold values from -3 to 3
- c_proj: bfloat16 [16, 1024], P(None, 'seq'), may hold values from -3 to 3
- log_decay: bfloat16 [25, 1024], P(None, 'seq'), may hold values from -1 to 0
- d_skip: float32 [1600], P('tp'), may hold values from 0.5 to 1.5
- entry_state: float32 [16, 1600], P(None, 'tp'), may hold values from -6 to 6
- doc_start: int32 [1024], P('seq'), may hold values 0 or 1
Outputs:
- input_grad: bfloat16 [1024, 1600], P(('seq', 'tp'))
- b_grad: float32 [16, 1024], P(None, 'seq')
- c_grad: float32 [16, 1024], P(None, 'seq')
The draws below stay inside these ranges and needn't reach their ends.
All inputs are finite; a program needn't handle non-finite values. No bound on the sum of `doc_start` on one device may be relied on, other than what follows from the above.
Results may differ from the reference program's by a relative error of at most 0.0065.
Values may be sent and summed in bfloat16 or wider, within the bound.
No kernel may reach another device: no remote copies, remote signals or barrier semaphores. Data moves between devices by JAX's collectives and lax.ppermute only.
A program may use at most 128 MiB of HBM per device.

```python
import math
import jax
import jax.numpy as jnp
from jax import lax

D = 1600
STATE = 16
RECURRENT_HEADS = 25
HDIM = 64
TOK_DEV = 128
TOKENS = 1024
INNER = 1600


def draw_log_decay(key, part):
    key = jax.random.fold_in(key, 7)
    random_subkeys = jax.random.split(key, 5)
    shape_power = 1.0
    slowest = 0.5 / TOKENS
    fastest = 1.0 / 30.0
    picked = jax.random.uniform(random_subkeys[0], (RECURRENT_HEADS,), jnp.float32) ** shape_power
    step_rates = jnp.exp(math.log(slowest) + (math.log(fastest) - math.log(slowest)) * picked)
    spread = math.log(2.0)
    roughness = jnp.exp(jax.random.uniform(random_subkeys[1], (RECURRENT_HEADS, TOKENS), jnp.float32, -spread, spread))
    device_part = jnp.exp(jax.random.uniform(random_subkeys[2], (RECURRENT_HEADS, TOKENS // TOK_DEV, 1), jnp.float32, -spread, spread))
    device_part = jnp.broadcast_to(device_part, (RECURRENT_HEADS, TOKENS // TOK_DEV, TOK_DEV)).reshape(RECURRENT_HEADS, TOKENS)
    rate_logarithms = -step_rates[:, None] * roughness * device_part
    fourth_part = TOKENS // 4
    sudden_rows = jnp.arange(4, dtype=jnp.int32)[None, :] * fourth_part + jax.random.randint(random_subkeys[3], (RECURRENT_HEADS, 4), 0, fourth_part)
    loss_values = jax.random.uniform(random_subkeys[4], (RECURRENT_HEADS, 4), jnp.float32, 0.2, 0.5)
    rows_per_head = jnp.broadcast_to(jnp.arange(RECURRENT_HEADS, dtype=jnp.int32)[:, None], (RECURRENT_HEADS, 4))
    rate_logarithms = rate_logarithms.at[rows_per_head, sudden_rows].add(jnp.log1p(-loss_values))
    return rate_logarithms.astype(jnp.bfloat16)


def touch_ends(values, rng, low, top_value):
    longest = values.shape.index(max(values.shape))
    spots = []
    for shift in (0, 1):
        where = [jax.random.randint(jax.random.fold_in(rng, axis), (), 0, length) for axis, length in enumerate(values.shape)]
        where[longest] = (where[longest] + shift) % values.shape[longest]
        spots.append(tuple(where))
    return values.at[spots[0]].set(low).at[spots[1]].set(top_value)


def block_levels(own_key, shape, cuts, smallest, high):
    factor_of, own = 1.0, jax.random.fold_in(own_key, 6)
    for axis_at, parts in cuts:
        steps = jnp.exp(jax.random.uniform(jax.random.fold_in(own, axis_at), (parts,), jnp.float32, smallest / len(cuts), high / len(cuts)))
        factor_of = factor_of * jnp.repeat(steps, shape[axis_at] // parts).reshape([-1 if axis == axis_at else 1 for axis in range(len(shape))])
    return factor_of


def normal_values(stream_key, shape, scale, bound, cuts=(), held_as=jnp.bfloat16):
    array = scale * jax.random.normal(stream_key, shape, jnp.float32)
    if cuts:
        array = array * block_levels(stream_key, shape, cuts, -0.22, 0.18)
    return jnp.clip(array, -bound, bound).astype(held_as)


def setup_inputs(seed: int = 0) -> dict:
    seeds = jax.random.split(jax.random.key(seed), 12)
    return {
        "layer_input": normal_values(seeds[0], (TOKENS, D), 1.0, 6.0, ((0, 32),)),
        "out_grad": normal_values(seeds[1], (TOKENS, D), 0.3, 2.5, ((0, 32),)),
        "w_in": normal_values(seeds[2], (INNER, D), D ** -0.5, 0.15625, ((0, 4),)),
        "w_gate": normal_values(seeds[3], (INNER, D), D ** -0.5, 0.15625, ((0, 4),)),
        "w_out": normal_values(seeds[4], (INNER, D), INNER ** -0.5, 0.15625, ((0, 4),)),
        "b_proj": normal_values(seeds[5], (STATE, TOKENS), 0.5, 3.0, ((1, 8),)),
        "c_proj": normal_values(seeds[6], (STATE, TOKENS), 0.5, 3.0, ((1, 8),)),
        "log_decay": draw_log_decay(jax.random.fold_in(seeds[11], 71), 0),
        "d_skip": jnp.clip(0.5 + 1.0 * jax.random.uniform(seeds[8], (INNER,), jnp.float32) ** block_levels(seeds[8], (INNER,), ((0, 4),), -0.2, 0.2), 0.5, 1.5),
        "entry_state": normal_values(seeds[9], (STATE, INNER), 1.0, 6.0, ((1, 4),), jnp.float32),
        "doc_start": touch_ends((jax.random.randint(seeds[10], (TOKENS,), 0, TOKENS // 8) < 1).astype(jnp.int32), jax.random.fold_in(seeds[10], 1), 0, 1),
    }


FULL_PRECISION = lax.Precision.HIGHEST

def silu_slope(values):
    logistic = jax.nn.sigmoid(values)
    return logistic * (1.0 + values * (1.0 - logistic))

def reference(layer_input, out_grad, w_in, w_gate, w_out, b_proj, c_proj, log_decay, d_skip, entry_state, doc_start):
    pre_act = jnp.dot(layer_input, w_in.T, preferred_element_type=jnp.float32)
    gate_act = jnp.dot(layer_input, w_gate.T, preferred_element_type=jnp.float32)
    x_rows = jax.nn.silu(pre_act).astype(jnp.bfloat16)
    mix_grad = jnp.dot(out_grad, w_out.T, preferred_element_type=jnp.float32)
    y_grads = (mix_grad * jax.nn.silu(gate_act)).astype(jnp.bfloat16)
    log_keep = jnp.repeat(log_decay.astype(jnp.float32), HDIM, axis=0).T
    resets = jnp.concatenate([jnp.zeros((1,), jnp.int32), doc_start[1:].astype(jnp.int32)])
    fresh_rows = (resets == 1)[:, None]
    keep_rate = jnp.where(fresh_rows, 0.0, jnp.exp(log_keep)).astype(jnp.float32)
    input_scale = jnp.where(fresh_rows, 1.0, jnp.sqrt(-jnp.expm1(2.0 * log_keep))).astype(jnp.float32)
    inputs = x_rows.astype(jnp.float32) * input_scale
    grad_rows = y_grads.astype(jnp.float32)
    b_rows = b_proj.astype(jnp.float32).T
    c_rows = c_proj.astype(jnp.float32).T

    def forward(states, pieces):
        keep_t, input_t, b_t, c_t, grad_t = pieces
        states = keep_t[None, :] * states + b_t[:, None] * input_t[None, :]
        out_t = jnp.dot(c_t, states, precision=FULL_PRECISION)
        c_grad_t = jnp.dot(states, grad_t, precision=FULL_PRECISION)
        return (states, (out_t, c_grad_t))
    sequence = (keep_rate, inputs, b_rows, c_rows, grad_rows)
    start_state = entry_state.astype(jnp.float32)
    _, (ssm_part, c_grad) = lax.scan(forward, start_state, sequence)
    ssm_out = (ssm_part + d_skip[None, :] * x_rows.astype(jnp.float32)).astype(jnp.bfloat16)

    def backward(carried, pieces):
        keep_t, input_t, b_t, c_t, grad_t = pieces
        state_grad = c_t[:, None] * grad_t[None, :] + carried
        x_part_t = jnp.dot(b_t, state_grad, precision=FULL_PRECISION)
        b_grad_t = jnp.dot(state_grad, input_t, precision=FULL_PRECISION)
        return (keep_t[None, :] * state_grad, (x_part_t, b_grad_t))
    zero_state = jnp.zeros(entry_state.shape, jnp.float32)
    _, (x_part, b_grad) = lax.scan(backward, zero_state, sequence, reverse=True)
    x_grad = (x_part * input_scale + d_skip[None, :] * grad_rows).astype(jnp.bfloat16)
    pre_grad = (x_grad.astype(jnp.float32) * silu_slope(pre_act)).astype(jnp.bfloat16)
    gate_grad = (mix_grad * ssm_out.astype(jnp.float32) * silu_slope(gate_act)).astype(jnp.bfloat16)
    total_grad = jnp.dot(pre_grad, w_in, preferred_element_type=jnp.float32) + jnp.dot(gate_grad, w_gate, preferred_element_type=jnp.float32)
    return (total_grad.astype(jnp.bfloat16), b_grad.T, c_grad.T)
```

```python
import jax
import jax.numpy as jnp
from jax import lax
from jax.experimental import pallas as pl
from jax.experimental.pallas import tpu as pltpu
from jax.sharding import PartitionSpec as P

HDIM = 64
LANE = 128
SLOT = 32

F32 = jnp.float32
BF16 = jnp.bfloat16
NN = (((1,), (0,)), ((), ()))
NT = (((1,), (1,)), ((), ()))
TN = (((0,), (0,)), ((), ()))


def dot(left, right, dims=NN):
    return lax.dot_general(left, right, dims, preferred_element_type=F32)


def round_up(value, step):
    return -(-value // step) * step


def silu_slope(values):
    logistic = jax.nn.sigmoid(values)
    return logistic * (1.0 + values * (1.0 - logistic))


def iota(shape, axis):
    return lax.broadcasted_iota(jnp.int32, shape, axis)


def one_minus_exp(values):
    series = 1.0 + values * (1.0 / 7.0)
    for term in (6.0, 5.0, 4.0, 3.0, 2.0):
        series = 1.0 + values * (1.0 / term) * series
    return jnp.where(values > -0.35, -values * series, 1.0 - jnp.exp(values))


def document_counts(doc_ref):
    tokens = doc_ref.shape[1]
    rows, columns = iota((tokens, tokens), 0), iota((tokens, tokens), 1)
    first = (iota((1, tokens), 1) == 0) & (lax.axis_index("seq") == 0)
    mark_row = jnp.where(first, 0.0, doc_ref[...].astype(F32))
    mark_row = jnp.broadcast_to(mark_row, (tokens, tokens))
    mark_column = jnp.sum(jnp.where(rows == columns, mark_row, 0.0), axis=1, keepdims=True)
    count_column = jnp.sum(jnp.where(columns <= rows, mark_row, 0.0), axis=1, keepdims=True)
    count_row = jnp.sum(
        jnp.where(rows <= columns, jnp.broadcast_to(mark_column, (tokens, tokens)), 0.0),
        axis=0,
        keepdims=True,
    )
    return mark_column, count_column, count_row


def head_picker(heads, channels, width):
    lanes = iota((heads, width), 1)
    head = iota((heads, width), 0)
    start = lax.axis_index("tp") * channels
    low = head * HDIM - start
    owned = (lanes >= low) & (lanes < low + HDIM) & (lanes < channels)
    spare = lanes - channels
    listed = (spare == head) | (spare == head + SLOT)
    return jnp.where(owned | listed, 1.0, 0.0).astype(BF16)


def decays(log_ref, doc_ref, picker):
    tokens = log_ref.shape[1]
    mark_column, count_column, count_row = document_counts(doc_ref)
    log_rows = dot(log_ref[...], picker, TN)
    rows, columns = iota((tokens, tokens), 0), iota((tokens, tokens), 1)
    lower = jnp.where(columns <= rows, 1.0, 0.0).astype(BF16)
    cumulative = dot(lower, log_rows.astype(BF16))
    scale = jnp.where(mark_column == 1.0, 1.0, jnp.sqrt(one_minus_exp(2.0 * log_rows)))
    last_count = count_column[tokens - 1 : tokens, :]
    total = cumulative[tokens - 1 : tokens, :]
    centre = cumulative[tokens // 2 : tokens // 2 + 1, :]
    rising = jnp.exp(cumulative - centre)
    falling = jnp.exp(centre - cumulative)
    fresh = jnp.where(count_column == 0.0, 1.0, 0.0)
    inside = jnp.where(count_column == last_count, 1.0, 0.0)
    carry_in = jnp.exp(cumulative) * fresh
    carry_out = jnp.exp(total - cumulative) * inside
    factor = jnp.exp(total) * fresh[tokens - 1 : tokens, :]
    return count_column, count_row, scale, rising, falling, carry_in, carry_out, factor


def two_parts(values):
    high = values.astype(BF16)
    return high, (values - high.astype(F32)).astype(BF16)


def fine_dot(left, right, dims=NN):
    (left_high, left_low), (right_high, right_low) = two_parts(left), two_parts(right)
    small = dot(left_high, right_low, dims) + dot(left_low, right_high, dims)
    return dot(left_high, right_high, dims) + small


class Staged:
    def __init__(self, ins, outs, through, refs):
        refs = list(refs)
        far_in = [name for name, (_, far) in ins.items() if far is True and name not in through]
        far_out = [name for name, (_, _, far) in outs.items() if far]
        self.refs = {name: refs.pop(0) for name in ins}
        made = {name: refs.pop(0) for name in outs}
        held = {name: refs.pop(0) for name in far_in}
        self.made = dict(made, **{name: refs.pop(0) for name in far_out})
        sems = refs.pop(0) if far_in or far_out or through else None
        self.rest = refs
        self.loads = {
            name: pltpu.make_async_copy(self.refs[name], held[name], sems.at[at])
            for at, name in enumerate(far_in)
        }
        self.stores = {
            name: pltpu.make_async_copy(self.made[name], made[name], sems.at[len(far_in) + at])
            for at, name in enumerate(far_out)
        }
        self.passed = [
            pltpu.make_async_copy(self.refs[name], made[name], sems.at[len(far_in + far_out) + at])
            for at, name in enumerate(through)
        ]
        self.refs.update(held)
        for copy in (*self.loads.values(), *self.passed):
            copy.start()

    def take(self, name):
        if name in self.loads:
            self.loads.pop(name).wait()
        return self.refs[name]

    def put(self, name, value):
        self.made[name][...] = value
        self.send(name)

    def send(self, name):
        if name in self.stores:
            self.stores[name].start()

    def finish(self):
        for copy in (*self.stores.values(), *self.passed):
            copy.wait()


def pin(value):
    return pltpu.with_memory_space_constraint(value, pltpu.HBM)


def near(*values):
    return (*values, False)


def far(*values):
    return (*values, True)


def staged_call(body, name, ins, outs, flops=0, scratch=(), through=()):
    outs = dict(outs, **{name: near(ins[name][0].shape, ins[name][0].dtype) for name in through})

    def kernel(*refs):
        staged = Staged(ins, outs, through, refs)
        body(staged, *staged.rest)
        staged.finish()

    def spec(is_far):
        return pl.BlockSpec(memory_space=pltpu.HBM if is_far else pltpu.VMEM)

    held = [
        pltpu.VMEM(value.shape, value.dtype)
        for name, (value, is_far) in ins.items()
        if is_far is True and name not in through
    ]
    held += [pltpu.VMEM(shape, dtype) for shape, dtype, is_far in outs.values() if is_far]
    copies = len(held) + len(through)
    sems = [pltpu.SemaphoreType.DMA((copies,))] if copies else []
    results = pl.pallas_call(
        kernel,
        name=name,
        out_shape=[jax.ShapeDtypeStruct(shape, dtype) for shape, dtype, _ in outs.values()],
        in_specs=[spec(is_far) for _, is_far in ins.values()],
        out_specs=[spec(is_far) for _, _, is_far in outs.values()],
        scratch_shapes=held + sems + list(scratch),
        compiler_params=pltpu.CompilerParams(vmem_limit_bytes=24 * 2**20),
        cost_estimate=pl.CostEstimate(flops=flops, bytes_accessed=2**20, transcendentals=0),
    )(*[pin(value) if is_far else value for value, is_far in ins.values()])
    return dict(zip(outs, results))


def assemble(staged, name, whole):
    for step in range(whole.shape[0] // staged.refs[name + "0"].shape[0]):
        block = staged.take(name + "%d" % step)
        piece = block.shape[0]
        start = pl.multiple_of((lax.axis_index("tp") ^ step) * piece, piece)
        whole[pl.ds(start, piece), :] = block[...]


def head_expander(channels, width):
    first = channels // LANE * LANE
    shape = (width - first, width)
    slot = iota(shape, 0) + (first - channels)
    lane = iota(shape, 1)
    spare = lane - channels
    head = jnp.where(slot < SLOT, slot, slot - SLOT)
    low = head * HDIM - lax.axis_index("tp") * channels
    owned = (lane >= low) & (lane < low + HDIM) & (lane < channels)
    listed = (spare == head) | (spare == head + SLOT)
    kept = (slot >= 0) & (slot < 2 * SLOT)
    return jnp.where(kept & (owned | listed), 1.0, 0.0).astype(BF16)


def encode(value, factor, channels):
    lane = iota(value.shape, 1)
    high = factor.astype(BF16).astype(F32)
    listed = jnp.where(lane < channels + SLOT, high, factor - high)
    return jnp.where(lane < channels, value, listed).astype(BF16)


def decode(message, expander):
    return dot(message[:, message.shape[1] - expander.shape[0] :], expander)


def partner_is_later(bit):
    return lax.axis_index("seq") % (2 * bit) < bit


def put_message(staged, state_part, grad_part, factor, channels, bit):
    message = staged.made["message"]
    states = state_part.shape[0]
    if message.shape[0] == states:
        part = jnp.where(partner_is_later(bit), state_part, grad_part)
        message[...] = encode(part, factor, channels)
    else:
        message[:states, :] = encode(state_part, factor, channels)
        message[states:, :] = encode(grad_part, factor, channels)


def prepare(staged):
    tokens, channels = staged.made["enter"].shape
    width = staged.made["factor"].shape[1]
    log_ref = staged.take("log")
    picker = head_picker(log_ref.shape[0], channels, width)
    count_column, count_row, scale, rising, falling, carry_in, carry_out, factor = decays(
        log_ref, staged.take("doc"), picker
    )
    staged.put("enter", carry_in[:, :channels])
    staged.put("leave", (scale * carry_out)[:, :channels])
    staged.put("rise", rising[:, :channels])
    staged.put("fall", (scale * falling)[:, :channels])
    staged.put("factor", jnp.broadcast_to(factor, staged.made["factor"].shape))
    staged.put("expander", head_expander(channels, width))
    rows, columns = iota((tokens, tokens), 0), iota((tokens, tokens), 1)
    same = count_column == count_row
    causal = (rows >= columns) & same
    anticausal = (rows <= columns) & same
    b_rows, c_rows = staged.take("b_in")[...], staged.take("c_in")[...]
    staged.put("causal", jnp.where(causal, 1.0, 0.0))
    staged.put("crossed", jnp.where(causal, dot(c_rows, b_rows, TN), 0.0))
    staged.put("crossed_back", jnp.where(anticausal, dot(b_rows, c_rows, TN), 0.0))
    staged.put("b", b_rows)
    staged.put("c", c_rows)


def put_summary(staged, name, vectors, values):
    part = staged.made[name]
    part[...] = jnp.zeros_like(part)
    part[:, : values.shape[1]] = dot(staged.take(vectors)[...], values)


def project(staged, rows_ref):
    assemble(staged, "rows", rows_ref)
    rows = rows_ref[...]
    pre = dot(rows, staged.take("w_in")[...], NT)
    staged.put("pre", pre)
    x_rows = (pre * jax.nn.sigmoid(pre)).astype(BF16)
    staged.put("x", x_rows)
    leaving = (x_rows.astype(F32) * staged.take("leave")[...]).astype(BF16)
    staged.put("leaving", leaving)
    put_summary(staged, "state", "b", leaving)
    gate = dot(rows, staged.take("w_gate")[...], NT)
    staged.put("gate", gate)
    staged.put("gated", gate * jax.nn.sigmoid(gate))


def front(staged, grad_ref):
    channels = staged.made["mix"].shape[1]
    assemble(staged, "grad", grad_ref)
    mix = dot(grad_ref[...], staged.take("w_out")[...], NT)
    staged.put("mix", mix)
    y_grads = (mix * staged.take("gated")[...]).astype(BF16)
    staged.put("y", y_grads)
    entering = (y_grads.astype(F32) * staged.take("enter")[...]).astype(BF16)
    staged.put("entering", entering)
    put_summary(staged, "grad", "c", entering)
    state_part, grad_part = staged.take("state")[...], staged.made["grad"][...]
    put_message(staged, state_part, grad_part, staged.take("factor")[...], channels, 1)


def join(channels, bit):
    def body(staged):
        received, expander = staged.take("received"), staged.take("expander")[...]
        factor, state, grad = (staged.take(name)[...] for name in ("factor", "state", "grad"))
        states = state.shape[0]
        other_state = received[:states, :].astype(F32)
        other_grad = received[states:, :].astype(F32)
        other = decode(received[:states, :], expander)
        later = partner_is_later(bit)
        if bit == 1:
            before = jnp.where(later, 1.0, other), jnp.where(later, 0.0, other_state)
            behind = jnp.where(later, other, 1.0), jnp.where(later, other_grad, 0.0)
        else:
            keep, held, back_keep, back_held = (
                staged.take(name)[...] for name in ("keep", "held", "back_keep", "back_held")
            )
            before = (
                jnp.where(later, keep, keep * other),
                jnp.where(later, held, keep * other_state + held),
            )
            behind = (
                jnp.where(later, back_keep * other, back_keep),
                jnp.where(later, back_keep * other_grad + back_held, back_held),
            )
        staged.put("keep", before[0])
        staged.put("held", before[1])
        staged.put("back_keep", behind[0])
        staged.put("back_held", behind[1])
        joined_state = jnp.where(later, other * state + other_state, factor * other_state + state)
        joined_grad = jnp.where(later, grad + factor * other_grad, other_grad + other * grad)
        joined = factor * other
        put_message(staged, joined_state, joined_grad, joined, channels, 2 * bit)
        if "state" in staged.made:
            staged.put("state", joined_state)
            staged.put("grad", joined_grad)
            staged.put("factor", joined)

    return body


def slopes(staged):
    staged.put("pre_slope", silu_slope(staged.take("pre")[...]))
    staged.put("gate_slope", staged.take("mix")[...] * silu_slope(staged.take("gate")[...]))


def local_vectors(staged):
    upper = staged.take("y")[...].astype(F32) * staged.take("rise")[...]
    lower = staged.take("x")[...].astype(F32) * staged.take("fall")[...]
    causal = staged.take("causal")[...] > 0.0
    high, low = two_parts(jnp.where(causal, fine_dot(upper, lower, NT), 0.0))
    b_rows, c_rows = staged.take("b")[...], staged.take("c")[...]
    states = b_rows.shape[0]
    bc = staged.made["bc"]
    bc[:states, :] = dot(c_rows, high) + dot(c_rows, low)
    bc[states:, :] = dot(b_rows, high, NT) + dot(b_rows, low, NT)


def local_channels(staged):
    x_rows, y_grads = staged.take("x")[...].astype(F32), staged.take("y")[...].astype(F32)
    rise, fall, skip = staged.take("rise")[...], staged.take("fall")[...], staged.take("skip")[...]
    ssm = rise * fine_dot(staged.take("crossed")[...], x_rows * fall)
    staged.put("ssm", ssm + skip * x_rows)
    x_grad = fall * fine_dot(staged.take("crossed_back")[...], y_grads * rise)
    staged.put("x_grad", x_grad + skip * y_grads)


def put_pieces(staged, steps, gate_rows, pre_rows, bc):
    piece = gate_rows.shape[0] // len(steps)
    partial = dot(gate_rows, staged.take("w_gate")[...])
    partial += dot(pre_rows, staged.take("w_in")[...])
    depth = partial.shape[1]
    for at, step in enumerate(steps):
        made = staged.made["part%d" % step]
        split = made.shape[1] - bc.shape[1]
        if split > depth:
            made[:, split - LANE : split] = jnp.zeros((piece, LANE), made.dtype)
        made[:, :depth] = partial[at * piece : (at + 1) * piece, :].astype(made.dtype)
        made[: bc.shape[0], split:] = bc.astype(made.dtype)


def back(bit, urgent, later_steps):
    def body(staged, gate_ref, pre_ref):
        entry = staged.take("entry")[...]
        states, channels = entry.shape
        received = staged.take("received")
        other_part = received[:, :channels].astype(F32)
        other = decode(received[...], staged.take("expander")[...])[:, :channels]
        later = partner_is_later(bit)
        keep, held, back_keep, back_held = (
            staged.take(name)[:, :channels] for name in ("keep", "held", "back_keep", "back_held")
        )
        state = jnp.where(later, entry, other * entry + other_part)
        state_in = (keep * state + held).astype(BF16)
        grad_in = jnp.where(later, back_keep * other_part + back_held, back_held).astype(BF16)
        carried = dot(staged.take("c")[...], state_in, TN)
        ssm_out = staged.take("ssm")[...] + staged.take("enter")[...] * carried
        gate_ref[...] = (
            ssm_out.astype(BF16).astype(F32) * staged.take("gate_slope")[...]
        ).astype(BF16)
        carried = dot(staged.take("b")[...], grad_in, TN)
        x_grad = staged.take("x_grad")[...] + staged.take("leave")[...] * carried
        pre_ref[...] = (
            x_grad.astype(BF16).astype(F32) * staged.take("pre_slope")[...]
        ).astype(BF16)
        bc = staged.made["bc"]
        local = staged.take("bc")
        bc[:states, :] = local[:states, :] + dot(grad_in, staged.take("leaving")[...], NT)
        bc[states:, :] = local[states:, :] + dot(state_in, staged.take("entering")[...], NT)
        piece = gate_ref.shape[0] // len(urgent + later_steps)

        def gathered(ref, steps):
            tp = lax.axis_index("tp")
            starts = [pl.multiple_of((tp ^ step) * piece, piece) for step in steps]
            return jnp.concatenate([ref[pl.ds(start, piece), :] for start in starts], axis=0)

        staged.put("gate_rows", gathered(gate_ref, later_steps))
        staged.put("pre_rows", gathered(pre_ref, later_steps))
        put_pieces(staged, urgent, gathered(gate_ref, urgent), gathered(pre_ref, urgent), bc[...])

    return body


def rest(steps):
    def body(staged):
        gate_rows, pre_rows = staged.take("gate_rows")[...], staged.take("pre_rows")[...]
        put_pieces(staged, steps, gate_rows, pre_rows, staged.take("bc")[...])

    return body


def add(staged):
    values = [staged.take(name)[...].astype(F32) for name in staged.refs]
    staged.put("sum", sum(values).astype(BF16))


def total(staged):
    depth = staged.made["grad"].shape[1]
    states, tokens = staged.made["b"].shape
    received = [staged.take(name) for name in staged.refs]
    split = received[0].shape[1] - tokens
    staged.put("grad", sum(part[:, :depth].astype(F32) for part in received).astype(BF16))
    staged.put("b", sum(part[:states, split:].astype(F32) for part in received))
    staged.put("c", sum(part[states : 2 * states, split:].astype(F32) for part in received))


def swap_masks(parts):
    masks, bit = [], parts // 2
    while bit:
        masks.append(bit)
        bit //= 2
    return masks


def reached(masks):
    steps = {0}
    for mask in masks:
        steps |= {step ^ mask for step in steps}
    return steps


def shards(
    layer_input, out_grad, w_in, w_gate, w_out, b_proj, c_proj, log_decay, d_skip, entry_state,
    doc_start,
):
    owners, parts = lax.axis_size("seq"), lax.axis_size("tp")
    assert owners > 2 and owners & (owners - 1) == 0 and parts & (parts - 1) == 0
    piece, depth = layer_input.shape
    tokens = piece * parts
    channels = w_in.shape[0]
    states = b_proj.shape[0]
    width = round_up(channels + 2 * SLOT, LANE)
    wide = near((tokens, channels), F32)
    half = near((tokens, channels), BF16)
    square = near((tokens, tokens), F32)
    row = near((states, tokens), BF16)
    summary = near((states, width), F32)

    def ordered(value, after):
        return lax.optimization_barrier((value, after))[0]

    def swap(value, axis, bit):
        size = lax.axis_size(axis)
        return lax.ppermute(value, axis, [(at, at ^ bit) for at in range(size)])

    def call(body, name, ins, outs, **options):
        ins = {key: near(value) if hasattr(value, "shape") else value for key, value in ins.items()}
        return staged_call(body, name, ins, outs, **options)

    def pick(source, names):
        return {name: source[name] for name in names}

    far_ins = dict(
        log=log_decay, doc=doc_start.reshape(1, tokens), b_in=b_proj, c_in=c_proj, w_gate=w_gate,
        w_in=w_in, w_out=w_out, rows0=layer_input, grad0=out_grad, entry=entry_state,
        skip=d_skip.reshape(1, channels),
    )
    ready = call(
        prepare, "prepare", {name: far(value) for name, value in far_ins.items()},
        dict(enter=wide, leave=wide, rise=wide, fall=wide, factor=summary,
             expander=near((width - channels // LANE * LANE, width), BF16), causal=square,
             crossed=square, crossed_back=square, b=row, c=row),
        flops=8 * tokens * channels * tokens,
        through=("w_gate", "w_in", "w_out", "rows0", "grad0", "entry", "skip"),
    )
    grad_blocks, row_blocks = {0: out_grad}, {0: layer_input}
    masks = swap_masks(parts)
    for mask in masks:
        for blocks in (row_blocks, grad_blocks):
            for step in list(blocks):
                block = blocks[step]
                if mask != masks[0]:
                    block = ordered(block, ready["expander"])
                blocks[step ^ mask] = swap(block, "tp", mask)
    rows = {"rows%d" % step: block for step, block in row_blocks.items()}
    grads = {"grad%d" % step: block for step, block in grad_blocks.items()}
    rows["rows0"], grads["grad0"] = ready["rows0"], ready["grad0"]
    assembled = pltpu.VMEM((tokens, depth), BF16)
    both = near((2 * states, width), BF16)
    one = near((states, width), BF16)
    first = call(
        project, "project",
        dict(rows, **pick(ready, ("w_gate", "w_in", "b", "leave"))),
        dict(gate=wide, gated=wide, pre=wide, x=half, leaving=half, state=summary),
        flops=4 * tokens * channels * depth, scratch=(assembled,),
    )
    first.update(call(
        front, "front",
        dict(grads, **pick(ready, ("w_out", "c", "enter", "factor")),
             **pick(first, ("gated", "state"))),
        dict(mix=wide, y=half, entering=half, grad=summary, message=both),
        flops=2 * tokens * channels * depth, scratch=(assembled,),
    ))
    group = dict(pick(first, ("state", "grad")), factor=ready["factor"])
    received = swap(first["message"], "seq", 1)
    slope = call(
        slopes, "slopes", pick(first, ("pre", "gate", "mix")),
        dict(pre_slope=wide, gate_slope=wide), flops=tokens * channels * 32,
    )
    received = ordered(received, slope["pre_slope"])
    x_rows, y_grads = first["x"], first["y"]
    results, bit = {}, 1
    while 2 * bit < owners:
        last = 4 * bit >= owners
        outs = dict(keep=summary, held=summary, back_keep=summary, back_held=summary,
                    message=one if last else both)
        if not last:
            outs.update(state=summary, grad=summary, factor=summary)
        group = call(
            join(channels, bit), "join", dict(group, received=received, expander=ready["expander"]),
            outs,
        )
        received = swap(group.pop("message"), "seq", 2 * bit)
        if bit == 1:
            results.update(call(
                local_vectors, "local_vectors",
                dict(pick(ready, ("rise", "fall", "causal", "b", "c")),
                     x=ordered(x_rows, group["keep"]), y=y_grads),
                dict(bc=near((2 * states, tokens), F32)), flops=8 * tokens * channels * tokens,
            ))
            if not last:
                received = ordered(received, results["bc"])
        if last:
            results.update(call(
                local_channels, "local_channels",
                dict(pick(ready, ("rise", "fall", "crossed", "crossed_back", "skip")),
                     x=ordered(x_rows, group["keep"]), y=y_grads),
                dict(ssm=wide, x_grad=wide), flops=16 * tokens * channels * tokens,
            ))
        bit *= 2
    span = round_up(depth, LANE) + tokens
    graded = pltpu.VMEM((tokens, channels), BF16)
    kept = reached(masks[:-1])
    urgent = sorted(set(range(parts)) - kept - {masks[-1]})
    others = sorted(set(range(parts)) - set(urgent))
    pieces = {"part%d" % step: near((piece, span), F32 if step in kept else BF16)
              for step in range(parts)}
    rest_rows = near((piece * len(others), channels), BF16)
    held = call(
        back(bit, urgent, others), "back",
        dict(group, received=received, **results, **slope, **pick(first, ("entering", "leaving")),
             **pick(ready, ("entry", "expander", "enter", "leave", "b", "c", "w_gate", "w_in"))),
        dict(pick(pieces, ["part%d" % step for step in urgent]), gate_rows=rest_rows,
             pre_rows=rest_rows, bc=near((2 * states, tokens), F32)),
        flops=4 * len(urgent) * piece * channels * depth, scratch=(graded, graded),
    )
    held.update(call(
        rest(others), "rest",
        dict(pick(held, ("gate_rows", "pre_rows", "bc")), **pick(ready, ("w_gate", "w_in"))),
        pick(pieces, ["part%d" % step for step in others]),
        flops=4 * len(others) * piece * channels * depth,
    ))
    terms = {step: [held["part%d" % step]] for step in range(parts)}

    def summed(values):
        if len(values) == 1:
            return values[0]
        ins = {"term%d" % at: value for at, value in enumerate(values)}
        return call(add, "add", ins, dict(sum=near((piece, span), BF16)))["sum"]

    for level in reversed(range(len(masks))):
        for step in sorted(set(terms) - reached(masks[:level]), reverse=True):
            terms[step ^ masks[level]].append(swap(summed(terms.pop(step)), "tp", masks[level]))
    result = call(
        total, "total", {"term%d" % at: value for at, value in enumerate(terms[0])},
        dict(grad=near((piece, depth), BF16), b=near((states, tokens), F32),
             c=near((states, tokens), F32)),
    )
    return result["grad"], result["b"], result["c"]


def solution(mesh):
    in_specs = (
        P(("seq", "tp"), None),
        P(("seq", "tp"), None),
        P("tp", None),
        P("tp", None),
        P("tp", None),
        P(None, "seq"),
        P(None, "seq"),
        P(None, "seq"),
        P("tp"),
        P(None, "tp"),
        P("seq"),
    )
    out_specs = (P(("seq", "tp"), None), P(None, "seq"), P(None, "seq"))
    return jax.shard_map(shards, mesh=mesh, in_specs=in_specs, out_specs=out_specs, check_vma=False)
```

```python
import jax
import jax.numpy as jnp
from jax import lax
from jax.experimental import pallas as pl
from jax.experimental.pallas import tpu as pltpu
from jax.sharding import PartitionSpec as P

HDIM = 64
LANE = 128
SLOT = 32
SEQ, TP = "seq", "tp"

F32 = jnp.float32
BF16 = jnp.bfloat16
NN = (((1,), (0,)), ((), ()))
NT = (((1,), (1,)), ((), ()))
TN = (((0,), (0,)), ((), ()))


def dot(left, right, dims=NN):
    return lax.dot_general(left, right, dims, preferred_element_type=F32)


def round_up(value, step):
    return -(-value // step) * step


def silu_slope(values):
    logistic = jax.nn.sigmoid(values)
    return logistic * (1.0 + values * (1.0 - logistic))


def iota(shape, axis):
    return lax.broadcasted_iota(jnp.int32, shape, axis)


def one_minus_exp(values):
    series = 1.0 + values * (1.0 / 7.0)
    for term in (6.0, 5.0, 4.0, 3.0, 2.0):
        series = 1.0 + values * (1.0 / term) * series
    return jnp.where(values > -0.35, -values * series, 1.0 - jnp.exp(values))


def document_counts(doc_ref):
    tokens = doc_ref.shape[1]
    rows, columns = iota((tokens, tokens), 0), iota((tokens, tokens), 1)
    first = (iota((1, tokens), 1) == 0) & (lax.axis_index(SEQ) == 0)
    mark_row = jnp.where(first, 0.0, doc_ref[...].astype(F32))
    mark_row = jnp.broadcast_to(mark_row, (tokens, tokens))
    mark_column = jnp.sum(jnp.where(rows == columns, mark_row, 0.0), axis=1, keepdims=True)
    count_column = jnp.sum(jnp.where(columns <= rows, mark_row, 0.0), axis=1, keepdims=True)
    count_row = jnp.sum(
        jnp.where(rows <= columns, jnp.broadcast_to(mark_column, (tokens, tokens)), 0.0),
        axis=0,
        keepdims=True,
    )
    return mark_column, count_column, count_row


def head_picker(heads, channels, width):
    lanes = iota((heads, width), 1)
    head = iota((heads, width), 0)
    start = lax.axis_index(TP) * channels
    low = head * HDIM - start
    owned = (lanes >= low) & (lanes < low + HDIM) & (lanes < channels)
    spare = lanes - channels
    listed = (spare == head) | (spare == head + SLOT)
    return jnp.where(owned | listed, 1.0, 0.0).astype(BF16)


def decays(log_ref, doc_ref, picker):
    tokens = log_ref.shape[1]
    mark_column, count_column, count_row = document_counts(doc_ref)
    log_rows = dot(log_ref[...], picker, TN)
    rows, columns = iota((tokens, tokens), 0), iota((tokens, tokens), 1)
    lower = jnp.where(columns <= rows, 1.0, 0.0).astype(BF16)
    cumulative = dot(lower, log_rows.astype(BF16))
    scale = jnp.where(mark_column == 1.0, 1.0, jnp.sqrt(one_minus_exp(2.0 * log_rows)))
    last_count = count_column[tokens - 1 : tokens, :]
    total = cumulative[tokens - 1 : tokens, :]
    centre = cumulative[tokens // 2 : tokens // 2 + 1, :]
    rising = jnp.exp(cumulative - centre)
    falling = jnp.exp(centre - cumulative)
    fresh = jnp.where(count_column == 0.0, 1.0, 0.0)
    inside = jnp.where(count_column == last_count, 1.0, 0.0)
    carry_in = jnp.exp(cumulative) * fresh
    carry_out = jnp.exp(total - cumulative) * inside
    factor = jnp.exp(total) * fresh[tokens - 1 : tokens, :]
    return count_column, count_row, scale, rising, falling, carry_in, carry_out, factor


def two_parts(values):
    high = values.astype(BF16)
    return high, (values - high.astype(F32)).astype(BF16)


def fine_dot(left, right, dims=NN):
    (left_high, left_low), (right_high, right_low) = two_parts(left), two_parts(right)
    small = dot(left_high, right_low, dims) + dot(left_low, right_high, dims)
    return dot(left_high, right_high, dims) + small


class Values(dict):
    __getattr__ = dict.__getitem__


class Staged:
    def __init__(self, ins, outs, through, refs):
        refs = list(refs)
        far_in = [name for name, (_, far) in ins.items() if far is True and name not in through]
        far_out = [name for name, (_, _, far) in outs.items() if far]
        self.refs = {name: refs.pop(0) for name in ins}
        made = {name: refs.pop(0) for name in outs}
        held = {name: refs.pop(0) for name in far_in}
        self.made = Values(made, **{name: refs.pop(0) for name in far_out})
        sems = refs.pop(0) if far_in or far_out or through else None
        self.rest = refs
        self.loads = {
            name: pltpu.make_async_copy(self.refs[name], held[name], sems.at[at])
            for at, name in enumerate(far_in)
        }
        self.stores = {
            name: pltpu.make_async_copy(self.made[name], made[name], sems.at[len(far_in) + at])
            for at, name in enumerate(far_out)
        }
        self.passed = [
            pltpu.make_async_copy(self.refs[name], made[name], sems.at[len(far_in + far_out) + at])
            for at, name in enumerate(through)
        ]
        self.refs.update(held)
        for copy in (*self.loads.values(), *self.passed):
            copy.start()

    def take(self, name):
        if name in self.loads:
            self.loads.pop(name).wait()
        return self.refs[name]

    def __getattr__(self, name):
        return self.take(name)

    def put(self, **values):
        for name, value in values.items():
            self.made[name][...] = value
            self.send(name)

    def send(self, name):
        if name in self.stores:
            self.stores[name].start()

    def finish(self):
        for copy in (*self.stores.values(), *self.passed):
            copy.wait()


def pin(value):
    return pltpu.with_memory_space_constraint(value, pltpu.HBM)


def near(*values):
    return (*values, False)


def far(*values):
    return (*values, True)


def staged_call(body, ins, outs, flops=0, scratch=(), through=()):
    outs = dict(outs, **{name: near(ins[name][0].shape, ins[name][0].dtype) for name in through})

    def kernel(*refs):
        staged = Staged(ins, outs, through, refs)
        body(staged, *staged.rest)
        staged.finish()

    def spec(is_far):
        return pl.BlockSpec(memory_space=pltpu.HBM if is_far else pltpu.VMEM)

    held = [
        pltpu.VMEM(value.shape, value.dtype)
        for name, (value, is_far) in ins.items()
        if is_far is True and name not in through
    ]
    held += [pltpu.VMEM(shape, dtype) for shape, dtype, is_far in outs.values() if is_far]
    copies = len(held) + len(through)
    sems = [pltpu.SemaphoreType.DMA((copies,))] if copies else []
    results = pl.pallas_call(
        kernel,
        name=body.__name__,
        out_shape=[jax.ShapeDtypeStruct(shape, dtype) for shape, dtype, _ in outs.values()],
        in_specs=[spec(is_far) for _, is_far in ins.values()],
        out_specs=[spec(is_far) for _, _, is_far in outs.values()],
        scratch_shapes=held + sems + list(scratch),
        compiler_params=pltpu.CompilerParams(vmem_limit_bytes=24 * 2**20),
        cost_estimate=pl.CostEstimate(flops=flops, bytes_accessed=2**20, transcendentals=0),
    )(*[pin(value) if is_far else value for value, is_far in ins.values()])
    return Values(zip(outs, results))


def assemble(staged, name, whole):
    for step in range(whole.shape[0] // staged.refs[name + "0"].shape[0]):
        block = staged.take(name + "%d" % step)
        piece = block.shape[0]
        start = pl.multiple_of((lax.axis_index(TP) ^ step) * piece, piece)
        whole[pl.ds(start, piece), :] = block[...]


def head_expander(channels, width):
    first = channels // LANE * LANE
    shape = (width - first, width)
    slot = iota(shape, 0) + (first - channels)
    lane = iota(shape, 1)
    spare = lane - channels
    head = jnp.where(slot < SLOT, slot, slot - SLOT)
    low = head * HDIM - lax.axis_index(TP) * channels
    owned = (lane >= low) & (lane < low + HDIM) & (lane < channels)
    listed = (spare == head) | (spare == head + SLOT)
    kept = (slot >= 0) & (slot < 2 * SLOT)
    return jnp.where(kept & (owned | listed), 1.0, 0.0).astype(BF16)


def encode(value, factor, channels):
    lane = iota(value.shape, 1)
    high = factor.astype(BF16).astype(F32)
    listed = jnp.where(lane < channels + SLOT, high, factor - high)
    return jnp.where(lane < channels, value, listed).astype(BF16)


def decode(message, expander):
    return dot(message[:, message.shape[1] - expander.shape[0] :], expander)


def partner_is_later(bit):
    return lax.axis_index(SEQ) % (2 * bit) < bit


def put_message(staged, state_part, grad_part, factor, channels, bit):
    message = staged.made.message
    states = state_part.shape[0]
    if message.shape[0] == states:
        part = jnp.where(partner_is_later(bit), state_part, grad_part)
        message[...] = encode(part, factor, channels)
    else:
        message[:states, :] = encode(state_part, factor, channels)
        message[states:, :] = encode(grad_part, factor, channels)


def prepare(staged):
    tokens, channels = staged.made.enter.shape
    width = staged.made.factor.shape[1]
    log_ref = staged.log
    picker = head_picker(log_ref.shape[0], channels, width)
    count_column, count_row, scale, rising, falling, carry_in, carry_out, factor = decays(
        log_ref, staged.doc, picker
    )
    staged.put(enter=carry_in[:, :channels])
    staged.put(leave=(scale * carry_out)[:, :channels])
    staged.put(rise=rising[:, :channels])
    staged.put(fall=(scale * falling)[:, :channels])
    staged.put(factor=jnp.broadcast_to(factor, staged.made.factor.shape))
    staged.put(expander=head_expander(channels, width))
    rows, columns = iota((tokens, tokens), 0), iota((tokens, tokens), 1)
    same = count_column == count_row
    causal = (rows >= columns) & same
    anticausal = (rows <= columns) & same
    b_rows, c_rows = staged.b_in[...], staged.c_in[...]
    staged.put(causal=jnp.where(causal, 1.0, 0.0))
    staged.put(crossed=jnp.where(causal, dot(c_rows, b_rows, TN), 0.0))
    staged.put(crossed_back=jnp.where(anticausal, dot(b_rows, c_rows, TN), 0.0))
    staged.put(b=b_rows)
    staged.put(c=c_rows)


def put_summary(staged, name, vectors, values):
    part = staged.made[name]
    part[...] = jnp.zeros_like(part)
    part[:, : values.shape[1]] = dot(staged.take(vectors)[...], values)


def project(staged, rows_ref):
    assemble(staged, "rows", rows_ref)
    rows = rows_ref[...]
    pre = dot(rows, staged.w_in[...], NT)
    staged.put(pre=pre)
    x_rows = (pre * jax.nn.sigmoid(pre)).astype(BF16)
    staged.put(x=x_rows)
    leaving = (x_rows.astype(F32) * staged.leave[...]).astype(BF16)
    staged.put(leaving=leaving)
    put_summary(staged, "state", "b", leaving)
    gate = dot(rows, staged.w_gate[...], NT)
    staged.put(gate=gate)
    staged.put(gated=gate * jax.nn.sigmoid(gate))


def front(staged, grad_ref):
    channels = staged.made.mix.shape[1]
    assemble(staged, "grad", grad_ref)
    mix = dot(grad_ref[...], staged.w_out[...], NT)
    staged.put(mix=mix)
    y_grads = (mix * staged.gated[...]).astype(BF16)
    staged.put(y=y_grads)
    entering = (y_grads.astype(F32) * staged.enter[...]).astype(BF16)
    staged.put(entering=entering)
    put_summary(staged, "grad", "c", entering)
    state_part, grad_part = staged.state[...], staged.made.grad[...]
    put_message(staged, state_part, grad_part, staged.factor[...], channels, 1)


def join(channels, bit):
    def join_body(staged):
        received, expander = staged.received, staged.expander[...]
        factor, state, grad = (staged.take(name)[...] for name in ("factor", "state", "grad"))
        states = state.shape[0]
        other_state = received[:states, :].astype(F32)
        other_grad = received[states:, :].astype(F32)
        other = decode(received[:states, :], expander)
        later = partner_is_later(bit)
        if bit == 1:
            before = jnp.where(later, 1.0, other), jnp.where(later, 0.0, other_state)
            behind = jnp.where(later, other, 1.0), jnp.where(later, other_grad, 0.0)
        else:
            keep, held, back_keep, back_held = (
                staged.take(name)[...] for name in ("keep", "held", "back_keep", "back_held")
            )
            before = (
                jnp.where(later, keep, keep * other),
                jnp.where(later, held, keep * other_state + held),
            )
            behind = (
                jnp.where(later, back_keep * other, back_keep),
                jnp.where(later, back_keep * other_grad + back_held, back_held),
            )
        staged.put(keep=before[0])
        staged.put(held=before[1])
        staged.put(back_keep=behind[0])
        staged.put(back_held=behind[1])
        joined_state = jnp.where(later, other * state + other_state, factor * other_state + state)
        joined_grad = jnp.where(later, grad + factor * other_grad, other_grad + other * grad)
        joined = factor * other
        put_message(staged, joined_state, joined_grad, joined, channels, 2 * bit)
        if "state" in staged.made:
            staged.put(state=joined_state)
            staged.put(grad=joined_grad)
            staged.put(factor=joined)

    return join_body


def slopes(staged):
    staged.put(pre_slope=silu_slope(staged.pre[...]))
    staged.put(gate_slope=staged.mix[...] * silu_slope(staged.gate[...]))


def local_vectors(staged):
    upper = staged.y[...].astype(F32) * staged.rise[...]
    lower = staged.x[...].astype(F32) * staged.fall[...]
    causal = staged.causal[...] > 0.0
    high, low = two_parts(jnp.where(causal, fine_dot(upper, lower, NT), 0.0))
    b_rows, c_rows = staged.b[...], staged.c[...]
    states = b_rows.shape[0]
    bc = staged.made.bc
    bc[:states, :] = dot(c_rows, high) + dot(c_rows, low)
    bc[states:, :] = dot(b_rows, high, NT) + dot(b_rows, low, NT)


def local_channels(staged):
    x_rows, y_grads = staged.x[...].astype(F32), staged.y[...].astype(F32)
    rise, fall, skip = staged.rise[...], staged.fall[...], staged.skip[...]
    ssm = rise * fine_dot(staged.crossed[...], x_rows * fall)
    staged.put(ssm=ssm + skip * x_rows)
    x_grad = fall * fine_dot(staged.crossed_back[...], y_grads * rise)
    staged.put(x_grad=x_grad + skip * y_grads)


def back(bit):
    def back_body(staged, gate_ref, pre_ref):
        entry = staged.entry[...]
        states, channels = entry.shape
        received = staged.received
        other_part = received[:, :channels].astype(F32)
        other = decode(received[...], staged.expander[...])[:, :channels]
        later = partner_is_later(bit)
        keep, held, back_keep, back_held = (
            staged.take(name)[:, :channels] for name in ("keep", "held", "back_keep", "back_held")
        )
        state = jnp.where(later, entry, other * entry + other_part)
        state_in = (keep * state + held).astype(BF16)
        grad_in = jnp.where(later, back_keep * other_part + back_held, back_held).astype(BF16)
        carried = dot(staged.c[...], state_in, TN)
        ssm_out = staged.ssm[...] + staged.enter[...] * carried
        gate_ref[...] = (
            ssm_out.astype(BF16).astype(F32) * staged.gate_slope[...]
        ).astype(BF16)
        carried = dot(staged.b[...], grad_in, TN)
        x_grad = staged.x_grad[...] + staged.leave[...] * carried
        pre_ref[...] = (
            x_grad.astype(BF16).astype(F32) * staged.pre_slope[...]
        ).astype(BF16)
        local = staged.bc
        b_part = local[:states, :] + dot(grad_in, staged.leaving[...], NT)
        c_part = local[states:, :] + dot(state_in, staged.entering[...], NT)
        tokens = gate_ref.shape[0]
        kept, sent = staged.made.kept, staged.made.sent
        piece = tokens // (kept.shape[0] + sent.shape[0])
        count = kept.shape[0]
        tp = lax.axis_index(TP)
        steps = [2 * at for at in range(count)] + [2 * at + 1 for at in range(count)]
        starts = [pl.multiple_of((tp ^ step) * piece, piece) for step in steps]
        gate_rows, pre_rows = (
            jnp.concatenate([ref[pl.ds(start, piece), :] for start in starts], axis=0)
            for ref in (gate_ref, pre_ref)
        )
        partial = dot(gate_rows, staged.w_gate[...]) + dot(pre_rows, staged.w_in[...])
        depth = partial.shape[1]
        split = kept.shape[2] - tokens
        for at in range(2 * count):
            made, slot = (kept, at) if at < count else (sent, at - count)
            if split > depth:
                made[slot, :, split - LANE : split] = jnp.zeros((piece, LANE), made.dtype)
            made[slot, :, :depth] = partial[at * piece : (at + 1) * piece, :].astype(made.dtype)
            made[slot, :states, split:] = b_part.astype(made.dtype)
            made[slot, states : 2 * states, split:] = c_part.astype(made.dtype)

    return back_body


def add(staged):
    staged.put(far_sum=(staged.kept[1] + staged.arrived[1].astype(F32)).astype(BF16))


def total(staged):
    depth = staged.made.grad.shape[1]
    states, tokens = staged.made.b.shape
    split = staged.kept.shape[2] - tokens

    def summed(rows, lanes):
        own = staged.kept[0, rows, lanes] + staged.arrived[0, rows, lanes].astype(F32)
        return own + staged.far_sum[rows, lanes].astype(F32)

    staged.put(grad=summed(slice(None), slice(depth)).astype(BF16))
    staged.put(b=summed(slice(states), slice(split, None)))
    staged.put(c=summed(slice(states, 2 * states), slice(split, None)))


def swap_masks(parts):
    masks, bit = [], parts // 2
    while bit:
        masks.append(bit)
        bit //= 2
    return masks


def shards(
    layer_input, out_grad, w_in, w_gate, w_out, b_proj, c_proj, log_decay, d_skip, entry_state,
    doc_start,
):
    owners, parts = lax.axis_size(SEQ), lax.axis_size(TP)
    assert owners > 2 and owners & (owners - 1) == 0 and parts == 4
    piece, depth = layer_input.shape
    tokens = piece * parts
    channels = w_in.shape[0]
    states = b_proj.shape[0]
    width = round_up(channels + 2 * SLOT, LANE)
    wide = near((tokens, channels), F32)
    half = near((tokens, channels), BF16)
    square = near((tokens, tokens), F32)
    row = near((states, tokens), BF16)
    summary = near((states, width), F32)

    def ordered(value, after):
        return lax.optimization_barrier((value, after))[0]

    def swap(value, axis, bit):
        size = lax.axis_size(axis)
        return lax.ppermute(value, axis, [(at, at ^ bit) for at in range(size)])

    def call(body, ins, outs, **options):
        ins = {key: near(value) if hasattr(value, "shape") else value for key, value in ins.items()}
        return staged_call(body, ins, outs, **options)

    far_ins = dict(
        log=log_decay, doc=doc_start.reshape(1, tokens), b_in=b_proj, c_in=c_proj, w_gate=w_gate,
        w_in=w_in, w_out=w_out, rows0=layer_input, grad0=out_grad, entry=entry_state,
        skip=d_skip.reshape(1, channels),
    )
    ready = call(
        prepare, {name: far(value) for name, value in far_ins.items()},
        dict(enter=wide, leave=wide, rise=wide, fall=wide, factor=summary,
             expander=near((width - channels // LANE * LANE, width), BF16), causal=square,
             crossed=square, crossed_back=square, b=row, c=row),
        flops=8 * tokens * channels * tokens,
        through=("w_gate", "w_in", "w_out", "rows0", "grad0", "entry", "skip"),
    )
    grad_blocks, row_blocks = {0: out_grad}, {0: layer_input}
    masks = swap_masks(parts)
    for mask in masks:
        for blocks in (row_blocks, grad_blocks):
            for step in list(blocks):
                block = blocks[step]
                if mask != masks[0]:
                    block = ordered(block, ready.expander)
                blocks[step ^ mask] = swap(block, TP, mask)
    rows = {"rows%d" % step: block for step, block in row_blocks.items()}
    grads = {"grad%d" % step: block for step, block in grad_blocks.items()}
    rows["rows0"], grads["grad0"] = ready.rows0, ready.grad0
    assembled = pltpu.VMEM((tokens, depth), BF16)
    both = near((2 * states, width), BF16)
    one = near((states, width), BF16)
    first = call(
        project,
        dict(rows, **dict(w_gate=ready.w_gate, w_in=ready.w_in, b=ready.b, leave=ready.leave)),
        dict(gate=wide, gated=wide, pre=wide, x=half, leaving=half, state=summary),
        flops=4 * tokens * channels * depth, scratch=(assembled,),
    )
    first.update(call(
        front,
        dict(grads, **dict(w_out=ready.w_out, c=ready.c, enter=ready.enter, factor=ready.factor),
             **dict(gated=first.gated, state=first.state)),
        dict(mix=wide, y=half, entering=half, grad=summary, message=both),
        flops=2 * tokens * channels * depth, scratch=(assembled,),
    ))
    group = dict(dict(state=first.state, grad=first.grad), factor=ready.factor)
    received = swap(first.message, SEQ, 1)
    slope = call(
        slopes, dict(pre=first.pre, gate=first.gate, mix=first.mix),
        dict(pre_slope=wide, gate_slope=wide), flops=tokens * channels * 32,
    )
    received = ordered(received, slope.pre_slope)
    x_rows, y_grads = first.x, first.y
    results, bit = {}, 1
    while 2 * bit < owners:
        last = 4 * bit >= owners
        outs = dict(keep=summary, held=summary, back_keep=summary, back_held=summary,
                    message=one if last else both)
        if not last:
            outs.update(state=summary, grad=summary, factor=summary)
        group = call(
            join(channels, bit), dict(group, received=received, expander=ready.expander),
            outs,
        )
        received = swap(group.pop("message"), SEQ, 2 * bit)
        if bit == 1:
            results.update(call(
                local_vectors,
                dict(rise=ready.rise, fall=ready.fall, causal=ready.causal, b=ready.b, c=ready.c,
                     x=ordered(x_rows, group.keep), y=y_grads),
                dict(bc=near((2 * states, tokens), F32)), flops=8 * tokens * channels * tokens,
            ))
            if not last:
                received = ordered(received, results["bc"])
        if last:
            results.update(call(
                local_channels,
                dict(rise=ready.rise, fall=ready.fall, crossed=ready.crossed,
                     crossed_back=ready.crossed_back, skip=ready.skip,
                     x=ordered(x_rows, group.keep), y=y_grads),
                dict(ssm=wide, x_grad=wide), flops=16 * tokens * channels * tokens,
            ))
        bit *= 2
    span = round_up(depth, LANE) + tokens
    graded = pltpu.VMEM((tokens, channels), BF16)
    held = call(
        back(bit),
        dict(group, received=received, **results, **slope, entering=first.entering,
             leaving=first.leaving, entry=ready.entry, expander=ready.expander, enter=ready.enter,
             leave=ready.leave, b=ready.b, c=ready.c, w_gate=ready.w_gate, w_in=ready.w_in),
        dict(kept=near((parts // 2, piece, span), F32), sent=near((parts // 2, piece, span), BF16)),
        flops=4 * tokens * channels * depth, scratch=(graded, graded),
    )
    halves = dict(kept=held.kept, arrived=swap(held.sent, TP, 1))
    far_sum = call(add, halves, dict(far_sum=near((piece, span), BF16))).far_sum
    result = call(
        total, dict(halves, far_sum=swap(far_sum, TP, 2)),
        dict(grad=near((piece, depth), BF16), b=near((states, tokens), F32),
             c=near((states, tokens), F32)),
    )
    return result.grad, result.b, result.c


def solution(mesh):
    in_specs = (
        P((SEQ, TP), None),
        P((SEQ, TP), None),
        P(TP, None),
        P(TP, None),
        P(TP, None),
        P(None, SEQ),
        P(None, SEQ),
        P(None, SEQ),
        P(TP),
        P(None, TP),
        P(SEQ),
    )
    out_specs = (P((SEQ, TP), None), P(None, SEQ), P(None, SEQ))
    return jax.shard_map(shards, mesh=mesh, in_specs=in_specs, out_specs=out_specs, check_vma=False)
```

```python
import jax
import jax.numpy as jnp
from jax import lax
from jax.experimental import pallas as pl
from jax.experimental.pallas import tpu as pltpu
from jax.sharding import PartitionSpec as P

HDIM = 64
LANE = 128
SLOT = 32
SEQ, TP = "seq", "tp"

F32 = jnp.float32
BF16 = jnp.bfloat16
NN = (((1,), (0,)), ((), ()))
NT = (((1,), (1,)), ((), ()))
TN = (((0,), (0,)), ((), ()))


def dot(left, right, dims=NN):
    return lax.dot_general(left, right, dims, preferred_element_type=F32)


def round_up(value, step):
    return -(-value // step) * step


def silu_slope(values):
    logistic = jax.nn.sigmoid(values)
    return logistic * (1.0 + values * (1.0 - logistic))


def iota(shape, axis):
    return lax.broadcasted_iota(jnp.int32, shape, axis)


def one_minus_exp(values):
    series = 1.0 + values * (1.0 / 7.0)
    for term in (6.0, 5.0, 4.0, 3.0, 2.0):
        series = 1.0 + values * (1.0 / term) * series
    return jnp.where(values > -0.35, -values * series, 1.0 - jnp.exp(values))


def document_counts(doc_ref):
    tokens = doc_ref.shape[1]
    rows, columns = iota((tokens, tokens), 0), iota((tokens, tokens), 1)
    first = (iota((1, tokens), 1) == 0) & (lax.axis_index(SEQ) == 0)
    mark_row = jnp.where(first, 0.0, doc_ref[...].astype(F32))
    mark_row = jnp.broadcast_to(mark_row, (tokens, tokens))
    mark_column = jnp.sum(jnp.where(rows == columns, mark_row, 0.0), axis=1, keepdims=True)
    count_column = jnp.sum(jnp.where(columns <= rows, mark_row, 0.0), axis=1, keepdims=True)
    count_row = jnp.sum(
        jnp.where(rows <= columns, jnp.broadcast_to(mark_column, (tokens, tokens)), 0.0),
        axis=0,
        keepdims=True,
    )
    return mark_column, count_column, count_row


def head_picker(heads, channels, width):
    lanes = iota((heads, width), 1)
    head = iota((heads, width), 0)
    start = lax.axis_index(TP) * channels
    low = head * HDIM - start
    owned = (lanes >= low) & (lanes < low + HDIM) & (lanes < channels)
    spare = lanes - channels
    listed = (spare == head) | (spare == head + SLOT)
    return jnp.where(owned | listed, 1.0, 0.0).astype(BF16)


def decays(log_ref, doc_ref, picker):
    tokens = log_ref.shape[1]
    mark_column, count_column, count_row = document_counts(doc_ref)
    log_rows = dot(log_ref[...], picker, TN)
    rows, columns = iota((tokens, tokens), 0), iota((tokens, tokens), 1)
    lower = jnp.where(columns <= rows, 1.0, 0.0).astype(BF16)
    cumulative = dot(lower, log_rows.astype(BF16))
    scale = jnp.where(mark_column == 1.0, 1.0, jnp.sqrt(one_minus_exp(2.0 * log_rows)))
    last_count = count_column[tokens - 1 : tokens, :]
    total = cumulative[tokens - 1 : tokens, :]
    centre = cumulative[tokens // 2 : tokens // 2 + 1, :]
    rising = jnp.exp(cumulative - centre)
    falling = jnp.exp(centre - cumulative)
    fresh = jnp.where(count_column == 0.0, 1.0, 0.0)
    inside = jnp.where(count_column == last_count, 1.0, 0.0)
    carry_in = jnp.exp(cumulative) * fresh
    carry_out = jnp.exp(total - cumulative) * inside
    factor = jnp.exp(total) * fresh[tokens - 1 : tokens, :]
    return count_column, count_row, scale, rising, falling, carry_in, carry_out, factor


def two_parts(values):
    high = values.astype(BF16)
    return high, (values - high.astype(F32)).astype(BF16)


def fine_dot(left, right, dims=NN):
    (left_high, left_low), (right_high, right_low) = two_parts(left), two_parts(right)
    small = dot(left_high, right_low, dims) + dot(left_low, right_high, dims)
    return dot(left_high, right_high, dims) + small


class Values(dict):
    __getattr__ = dict.__getitem__


class Staged:
    def __init__(self, ins, outs, through, refs):
        refs = list(refs)
        far_in = [name for name, (_, far) in ins.items() if far is True and name not in through]
        far_out = [name for name, (_, _, far) in outs.items() if far]
        self.refs = {name: refs.pop(0) for name in ins}
        made = {name: refs.pop(0) for name in outs}
        held = {name: refs.pop(0) for name in far_in}
        self.made = Values(made, **{name: refs.pop(0) for name in far_out})
        sems = refs.pop(0) if far_in or far_out or through else None
        self.rest = refs
        self.loads = {
            name: pltpu.make_async_copy(self.refs[name], held[name], sems.at[at])
            for at, name in enumerate(far_in)
        }
        self.stores = {
            name: pltpu.make_async_copy(self.made[name], made[name], sems.at[len(far_in) + at])
            for at, name in enumerate(far_out)
        }
        self.passed = [
            pltpu.make_async_copy(self.refs[name], made[name], sems.at[len(far_in + far_out) + at])
            for at, name in enumerate(through)
        ]
        self.refs.update(held)
        for copy in (*self.loads.values(), *self.passed):
            copy.start()

    def take(self, name):
        if name in self.loads:
            self.loads.pop(name).wait()
        return self.refs[name]

    def __getattr__(self, name):
        return self.take(name)

    def put(self, **values):
        for name, value in values.items():
            self.made[name][...] = value
            self.send(name)

    def send(self, name):
        if name in self.stores:
            self.stores[name].start()

    def finish(self):
        for copy in (*self.stores.values(), *self.passed):
            copy.wait()


def pin(value):
    return pltpu.with_memory_space_constraint(value, pltpu.HBM)


def near(*values):
    return (*values, False)


def far(*values):
    return (*values, True)


def staged_call(body, ins, outs, flops=0, scratch=(), through=()):
    outs = dict(outs, **{name: near(ins[name][0].shape, ins[name][0].dtype) for name in through})

    def kernel(*refs):
        staged = Staged(ins, outs, through, refs)
        body(staged, *staged.rest)
        staged.finish()

    def spec(is_far):
        return pl.BlockSpec(memory_space=pltpu.HBM if is_far else pltpu.VMEM)

    held = [
        pltpu.VMEM(value.shape, value.dtype)
        for name, (value, is_far) in ins.items()
        if is_far is True and name not in through
    ]
    held += [pltpu.VMEM(shape, dtype) for shape, dtype, is_far in outs.values() if is_far]
    copies = len(held) + len(through)
    sems = [pltpu.SemaphoreType.DMA((copies,))] if copies else []
    results = pl.pallas_call(
        kernel,
        name=body.__name__,
        out_shape=[jax.ShapeDtypeStruct(shape, dtype) for shape, dtype, _ in outs.values()],
        in_specs=[spec(is_far) for _, is_far in ins.values()],
        out_specs=[spec(is_far) for _, _, is_far in outs.values()],
        scratch_shapes=held + sems + list(scratch),
        compiler_params=pltpu.CompilerParams(vmem_limit_bytes=24 * 2**20),
        cost_estimate=pl.CostEstimate(flops=flops, bytes_accessed=2**20, transcendentals=0),
    )(*[pin(value) if is_far else value for value, is_far in ins.values()])
    return Values(zip(outs, results))


def assemble(staged, name, whole):
    for step in range(whole.shape[0] // staged.refs[name + "0"].shape[0]):
        block = staged.take(name + "%d" % step)
        piece = block.shape[0]
        start = pl.multiple_of((lax.axis_index(TP) ^ step) * piece, piece)
        whole[pl.ds(start, piece), :] = block[...]


def head_expander(channels, width):
    first = channels // LANE * LANE
    shape = (width - first, width)
    slot = iota(shape, 0) + (first - channels)
    lane = iota(shape, 1)
    spare = lane - channels
    head = jnp.where(slot < SLOT, slot, slot - SLOT)
    low = head * HDIM - lax.axis_index(TP) * channels
    owned = (lane >= low) & (lane < low + HDIM) & (lane < channels)
    listed = (spare == head) | (spare == head + SLOT)
    kept = (slot >= 0) & (slot < 2 * SLOT)
    return jnp.where(kept & (owned | listed), 1.0, 0.0).astype(BF16)


def encode(value, factor, channels):
    lane = iota(value.shape, 1)
    high = factor.astype(BF16).astype(F32)
    listed = jnp.where(lane < channels + SLOT, high, factor - high)
    return jnp.where(lane < channels, value, listed).astype(BF16)


def decode(message, expander):
    return dot(message[:, message.shape[1] - expander.shape[0] :], expander)


def partner_is_later(bit):
    return lax.axis_index(SEQ) % (2 * bit) < bit


def put_message(staged, state_part, grad_part, factor, channels, bit):
    message = staged.made.message
    states = state_part.shape[0]
    if message.shape[0] == states:
        part = jnp.where(partner_is_later(bit), state_part, grad_part)
        message[...] = encode(part, factor, channels)
    else:
        message[:states, :] = encode(state_part, factor, channels)
        message[states:, :] = encode(grad_part, factor, channels)


def prepare(staged):
    tokens, channels = staged.made.enter.shape
    width = staged.made.factor.shape[1]
    log_ref = staged.log
    picker = head_picker(log_ref.shape[0], channels, width)
    count_column, count_row, scale, rising, falling, carry_in, carry_out, factor = decays(
        log_ref, staged.doc, picker
    )
    staged.put(enter=carry_in[:, :channels])
    staged.put(leave=(scale * carry_out)[:, :channels])
    staged.put(rise=rising[:, :channels])
    staged.put(fall=(scale * falling)[:, :channels])
    staged.put(factor=jnp.broadcast_to(factor, staged.made.factor.shape))
    staged.put(expander=head_expander(channels, width))
    rows, columns = iota((tokens, tokens), 0), iota((tokens, tokens), 1)
    same = count_column == count_row
    causal = (rows >= columns) & same
    anticausal = (rows <= columns) & same
    b_rows, c_rows = staged.b_in[...], staged.c_in[...]
    staged.put(causal=jnp.where(causal, 1.0, 0.0))
    staged.put(crossed=jnp.where(causal, dot(c_rows, b_rows, TN), 0.0))
    staged.put(crossed_back=jnp.where(anticausal, dot(b_rows, c_rows, TN), 0.0))
    staged.put(b=b_rows)
    staged.put(c=c_rows)


def put_summary(staged, name, vectors, values):
    part = staged.made[name]
    part[...] = jnp.zeros_like(part)
    part[:, : values.shape[1]] = dot(staged.take(vectors)[...], values)


def project(staged, rows_ref):
    assemble(staged, "rows", rows_ref)
    rows = rows_ref[...]
    pre = dot(rows, staged.w_in[...], NT)
    staged.put(pre=pre)
    x_rows = (pre * jax.nn.sigmoid(pre)).astype(BF16)
    staged.put(x=x_rows)
    leaving = (x_rows.astype(F32) * staged.leave[...]).astype(BF16)
    staged.put(leaving=leaving)
    put_summary(staged, "state", "b", leaving)
    gate = dot(rows, staged.w_gate[...], NT)
    staged.put(gate=gate)
    staged.put(gated=gate * jax.nn.sigmoid(gate))


def front(staged, grad_ref):
    channels = staged.made.mix.shape[1]
    assemble(staged, "grad", grad_ref)
    mix = dot(grad_ref[...], staged.w_out[...], NT)
    staged.put(mix=mix)
    y_grads = (mix * staged.gated[...]).astype(BF16)
    staged.put(y=y_grads)
    entering = (y_grads.astype(F32) * staged.enter[...]).astype(BF16)
    staged.put(entering=entering)
    put_summary(staged, "grad", "c", entering)
    state_part, grad_part = staged.state[...], staged.made.grad[...]
    put_message(staged, state_part, grad_part, staged.factor[...], channels, 1)


def join(channels, bit):
    def join_body(staged):
        received, expander = staged.received, staged.expander[...]
        factor, state, grad = (staged.take(name)[...] for name in ("factor", "state", "grad"))
        states = state.shape[0]
        other_state = received[:states, :].astype(F32)
        other_grad = received[states:, :].astype(F32)
        other = decode(received[:states, :], expander)
        later = partner_is_later(bit)
        if bit == 1:
            before = jnp.where(later, 1.0, other), jnp.where(later, 0.0, other_state)
            behind = jnp.where(later, other, 1.0), jnp.where(later, other_grad, 0.0)
        else:
            keep, held, back_keep, back_held = (
                staged.take(name)[...] for name in ("keep", "held", "back_keep", "back_held")
            )
            before = (
                jnp.where(later, keep, keep * other),
                jnp.where(later, held, keep * other_state + held),
            )
            behind = (
                jnp.where(later, back_keep * other, back_keep),
                jnp.where(later, back_keep * other_grad + back_held, back_held),
            )
        staged.put(keep=before[0])
        staged.put(held=before[1])
        staged.put(back_keep=behind[0])
        staged.put(back_held=behind[1])
        joined_state = jnp.where(later, other * state + other_state, factor * other_state + state)
        joined_grad = jnp.where(later, grad + factor * other_grad, other_grad + other * grad)
        joined = factor * other
        put_message(staged, joined_state, joined_grad, joined, channels, 2 * bit)
        if "state" in staged.made:
            staged.put(state=joined_state)
            staged.put(grad=joined_grad)
            staged.put(factor=joined)

    return join_body


def slopes(staged):
    staged.put(pre_slope=silu_slope(staged.pre[...]))
    staged.put(gate_slope=staged.mix[...] * silu_slope(staged.gate[...]))


def local_vectors(staged):
    upper = staged.y[...].astype(F32) * staged.rise[...]
    lower = staged.x[...].astype(F32) * staged.fall[...]
    causal = staged.causal[...] > 0.0
    high, low = two_parts(jnp.where(causal, fine_dot(upper, lower, NT), 0.0))
    b_rows, c_rows = staged.b[...], staged.c[...]
    states = b_rows.shape[0]
    bc = staged.made.bc
    bc[:states, :] = dot(c_rows, high) + dot(c_rows, low)
    bc[states:, :] = dot(b_rows, high, NT) + dot(b_rows, low, NT)


def local_channels(staged):
    x_rows, y_grads = staged.x[...].astype(F32), staged.y[...].astype(F32)
    rise, fall, skip = staged.rise[...], staged.fall[...], staged.skip[...]
    ssm = rise * fine_dot(staged.crossed[...], x_rows * fall)
    staged.put(ssm=ssm + skip * x_rows)
    x_grad = fall * fine_dot(staged.crossed_back[...], y_grads * rise)
    staged.put(x_grad=x_grad + skip * y_grads)


def put_pieces(staged, steps, gate_rows, pre_rows, bc):
    piece = gate_rows.shape[0] // len(steps)
    partial = dot(gate_rows, staged.w_gate[...])
    partial += dot(pre_rows, staged.w_in[...])
    depth = partial.shape[1]
    for at, step in enumerate(steps):
        made = staged.made["part%d" % step]
        split = made.shape[1] - bc.shape[1]
        if split > depth:
            made[:, split - LANE : split] = jnp.zeros((piece, LANE), made.dtype)
        made[:, :depth] = partial[at * piece : (at + 1) * piece, :].astype(made.dtype)
        made[: bc.shape[0], split:] = bc.astype(made.dtype)


def back(bit, urgent, later_steps):
    def back_body(staged, gate_ref, pre_ref):
        entry = staged.entry[...]
        states, channels = entry.shape
        received = staged.received
        other_part = received[:, :channels].astype(F32)
        other = decode(received[...], staged.expander[...])[:, :channels]
        later = partner_is_later(bit)
        keep, held, back_keep, back_held = (
            staged.take(name)[:, :channels] for name in ("keep", "held", "back_keep", "back_held")
        )
        state = jnp.where(later, entry, other * entry + other_part)
        state_in = (keep * state + held).astype(BF16)
        grad_in = jnp.where(later, back_keep * other_part + back_held, back_held).astype(BF16)
        carried = dot(staged.c[...], state_in, TN)
        ssm_out = staged.ssm[...] + staged.enter[...] * carried
        gate_ref[...] = (
            ssm_out.astype(BF16).astype(F32) * staged.gate_slope[...]
        ).astype(BF16)
        carried = dot(staged.b[...], grad_in, TN)
        x_grad = staged.x_grad[...] + staged.leave[...] * carried
        pre_ref[...] = (
            x_grad.astype(BF16).astype(F32) * staged.pre_slope[...]
        ).astype(BF16)
        bc = staged.made.bc
        local = staged.bc
        bc[:states, :] = local[:states, :] + dot(grad_in, staged.leaving[...], NT)
        bc[states:, :] = local[states:, :] + dot(state_in, staged.entering[...], NT)
        piece = gate_ref.shape[0] // len(urgent + later_steps)

        def gathered(ref, steps):
            tp = lax.axis_index(TP)
            starts = [pl.multiple_of((tp ^ step) * piece, piece) for step in steps]
            return jnp.concatenate([ref[pl.ds(start, piece), :] for start in starts], axis=0)

        staged.put(gate_rows=gathered(gate_ref, later_steps))
        staged.put(pre_rows=gathered(pre_ref, later_steps))
        put_pieces(staged, urgent, gathered(gate_ref, urgent), gathered(pre_ref, urgent), bc[...])

    return back_body


def rest(steps):
    def rest_body(staged):
        gate_rows, pre_rows = staged.gate_rows[...], staged.pre_rows[...]
        put_pieces(staged, steps, gate_rows, pre_rows, staged.bc[...])

    return rest_body


def add(staged):
    values = [staged.take(name)[...].astype(F32) for name in staged.refs]
    staged.put(sum=sum(values).astype(staged.made.sum.dtype))


def total(staged):
    depth = staged.made.grad.shape[1]
    states, tokens = staged.made.b.shape
    received = [staged.take(name) for name in staged.refs]
    split = received[0].shape[1] - tokens
    staged.put(grad=sum(part[:, :depth].astype(F32) for part in received).astype(BF16))
    staged.put(b=sum(part[:states, split:].astype(F32) for part in received))
    staged.put(c=sum(part[states : 2 * states, split:].astype(F32) for part in received))


def swap_masks(parts):
    masks, bit = [], parts // 2
    while bit:
        masks.append(bit)
        bit //= 2
    return masks


def shards(
    layer_input, out_grad, w_in, w_gate, w_out, b_proj, c_proj, log_decay, d_skip, entry_state,
    doc_start,
):
    owners, parts = lax.axis_size(SEQ), lax.axis_size(TP)
    assert owners > 2 and owners & (owners - 1) == 0 and parts == 4
    piece, depth = layer_input.shape
    tokens = piece * parts
    channels = w_in.shape[0]
    states = b_proj.shape[0]
    width = round_up(channels + 2 * SLOT, LANE)
    wide = near((tokens, channels), F32)
    half = near((tokens, channels), BF16)
    square = near((tokens, tokens), F32)
    row = near((states, tokens), BF16)
    summary = near((states, width), F32)

    def ordered(value, after):
        return lax.optimization_barrier((value, after))[0]

    def swap(value, axis, bit):
        size = lax.axis_size(axis)
        return lax.ppermute(value, axis, [(at, at ^ bit) for at in range(size)])

    def call(body, ins, outs, **options):
        ins = {key: near(value) if hasattr(value, "shape") else value for key, value in ins.items()}
        return staged_call(body, ins, outs, **options)

    far_ins = dict(
        log=log_decay, doc=doc_start.reshape(1, tokens), b_in=b_proj, c_in=c_proj, w_gate=w_gate,
        w_in=w_in, w_out=w_out, rows0=layer_input, grad0=out_grad, entry=entry_state,
        skip=d_skip.reshape(1, channels),
    )
    ready = call(
        prepare, {name: far(value) for name, value in far_ins.items()},
        dict(enter=wide, leave=wide, rise=wide, fall=wide, factor=summary,
             expander=near((width - channels // LANE * LANE, width), BF16), causal=square,
             crossed=square, crossed_back=square, b=row, c=row),
        flops=8 * tokens * channels * tokens,
        through=("w_gate", "w_in", "w_out", "rows0", "grad0", "entry", "skip"),
    )
    grad_blocks, row_blocks = {0: out_grad}, {0: layer_input}
    masks = swap_masks(parts)
    for mask in masks:
        for blocks in (row_blocks, grad_blocks):
            for step in list(blocks):
                block = blocks[step]
                if mask != masks[0]:
                    block = ordered(block, ready.expander)
                blocks[step ^ mask] = swap(block, TP, mask)
    rows = {"rows%d" % step: block for step, block in row_blocks.items()}
    grads = {"grad%d" % step: block for step, block in grad_blocks.items()}
    rows["rows0"], grads["grad0"] = ready.rows0, ready.grad0
    assembled = pltpu.VMEM((tokens, depth), BF16)
    both = near((2 * states, width), BF16)
    one = near((states, width), BF16)
    first = call(
        project,
        dict(rows, **dict(w_gate=ready.w_gate, w_in=ready.w_in, b=ready.b, leave=ready.leave)),
        dict(gate=wide, gated=wide, pre=wide, x=half, leaving=half, state=summary),
        flops=4 * tokens * channels * depth, scratch=(assembled,),
    )
    first.update(call(
        front,
        dict(grads, **dict(w_out=ready.w_out, c=ready.c, enter=ready.enter, factor=ready.factor),
             **dict(gated=first.gated, state=first.state)),
        dict(mix=wide, y=half, entering=half, grad=summary, message=both),
        flops=2 * tokens * channels * depth, scratch=(assembled,),
    ))
    group = dict(dict(state=first.state, grad=first.grad), factor=ready.factor)
    received = swap(first.message, SEQ, 1)
    slope = call(
        slopes, dict(pre=first.pre, gate=first.gate, mix=first.mix),
        dict(pre_slope=wide, gate_slope=wide), flops=tokens * channels * 32,
    )
    received = ordered(received, slope.pre_slope)
    x_rows, y_grads = first.x, first.y
    results, bit = {}, 1
    while 2 * bit < owners:
        last = 4 * bit >= owners
        outs = dict(keep=summary, held=summary, back_keep=summary, back_held=summary,
                    message=one if last else both)
        if not last:
            outs.update(state=summary, grad=summary, factor=summary)
        group = call(
            join(channels, bit), dict(group, received=received, expander=ready.expander),
            outs,
        )
        received = swap(group.pop("message"), SEQ, 2 * bit)
        if bit == 1:
            results.update(call(
                local_vectors,
                dict(rise=ready.rise, fall=ready.fall, causal=ready.causal, b=ready.b, c=ready.c,
                     x=ordered(x_rows, group.keep), y=y_grads),
                dict(bc=near((2 * states, tokens), F32)), flops=8 * tokens * channels * tokens,
            ))
            if not last:
                received = ordered(received, results["bc"])
        if last:
            results.update(call(
                local_channels,
                dict(rise=ready.rise, fall=ready.fall, crossed=ready.crossed,
                     crossed_back=ready.crossed_back, skip=ready.skip,
                     x=ordered(x_rows, group.keep), y=y_grads),
                dict(ssm=wide, x_grad=wide), flops=16 * tokens * channels * tokens,
            ))
        bit *= 2
    span = round_up(depth, LANE) + tokens
    graded = pltpu.VMEM((tokens, channels), BF16)
    kept, urgent, others = (0, 2), (2, 3), (0, 1)

    def named(steps):
        types = {step: F32 if step in kept else BF16 for step in steps}
        return {"part%d" % step: near((piece, span), types[step]) for step in steps}

    rest_rows = near((piece * len(others), channels), BF16)
    held = call(
        back(bit, urgent, others),
        dict(group, received=received, **results, **slope, entering=first.entering,
             leaving=first.leaving, entry=ready.entry, expander=ready.expander, enter=ready.enter,
             leave=ready.leave, b=ready.b, c=ready.c, w_gate=ready.w_gate, w_in=ready.w_in),
        dict(named(urgent), gate_rows=rest_rows,
             pre_rows=rest_rows, bc=near((2 * states, tokens), F32)),
        flops=4 * len(urgent) * piece * channels * depth, scratch=(graded, graded),
    )

    def added(dtype, one, two, **options):
        return call(add, dict(one=one, two=two), dict(sum=near((piece, span), dtype)), **options).sum

    far_sum = added(BF16, held.part2, swap(held.part3, TP, 1))
    distant = swap(far_sum, TP, 2)
    held.update(call(
        rest(others),
        dict(gate_rows=ordered(held.gate_rows, far_sum), pre_rows=held.pre_rows, bc=held.bc,
             w_gate=ready.w_gate, w_in=ready.w_in),
        named(others),
        flops=4 * len(others) * piece * channels * depth,
    ))
    own = added(F32, held.part0, distant, flops=tokens * channels * depth)
    result = call(
        total, dict(own=own, across=swap(held.part1, TP, 1)),
        dict(grad=near((piece, depth), BF16), b=near((states, tokens), F32),
             c=near((states, tokens), F32)),
    )
    return result.grad, result.b, result.c


def solution(mesh):
    in_specs = (
        P((SEQ, TP), None),
        P((SEQ, TP), None),
        P(TP, None),
        P(TP, None),
        P(TP, None),
        P(None, SEQ),
        P(None, SEQ),
        P(None, SEQ),
        P(TP),
        P(None, TP),
        P(SEQ),
    )
    out_specs = (P((SEQ, TP), None), P(None, SEQ), P(None, SEQ))
    return jax.shard_map(shards, mesh=mesh, in_specs=in_specs, out_specs=out_specs, check_vma=False)
```

```python
import jax
import jax.numpy as jnp
from jax import lax
from jax.experimental import pallas as pl
from jax.experimental.pallas import tpu as pltpu
from jax.sharding import PartitionSpec as P

HDIM = 64
LANE = 128
SLOT = 32
SEQ, TP = "seq", "tp"

F32 = jnp.float32
BF16 = jnp.bfloat16
NN = (((1,), (0,)), ((), ()))
NT = (((1,), (1,)), ((), ()))
TN = (((0,), (0,)), ((), ()))


def dot(left, right, dims=NN):
    return lax.dot_general(left, right, dims, preferred_element_type=F32)


def round_up(value, step):
    return -(-value // step) * step


def silu_slope(values):
    logistic = jax.nn.sigmoid(values)
    return logistic * (1.0 + values * (1.0 - logistic))


def iota(shape, axis):
    return lax.broadcasted_iota(jnp.int32, shape, axis)


def one_minus_exp(values):
    series = 1.0 + values * (1.0 / 7.0)
    for term in (6.0, 5.0, 4.0, 3.0, 2.0):
        series = 1.0 + values * (1.0 / term) * series
    return jnp.where(values > -0.35, -values * series, 1.0 - jnp.exp(values))


def document_counts(doc_ref):
    tokens = doc_ref.shape[1]
    rows, columns = iota((tokens, tokens), 0), iota((tokens, tokens), 1)
    first = (iota((1, tokens), 1) == 0) & (lax.axis_index(SEQ) == 0)
    mark_row = jnp.where(first, 0.0, doc_ref[...].astype(F32))
    mark_row = jnp.broadcast_to(mark_row, (tokens, tokens))
    mark_column = jnp.sum(jnp.where(rows == columns, mark_row, 0.0), axis=1, keepdims=True)
    count_column = jnp.sum(jnp.where(columns <= rows, mark_row, 0.0), axis=1, keepdims=True)
    count_row = jnp.sum(
        jnp.where(rows <= columns, jnp.broadcast_to(mark_column, (tokens, tokens)), 0.0),
        axis=0,
        keepdims=True,
    )
    return mark_column, count_column, count_row


def head_picker(heads, channels, width):
    lanes = iota((heads, width), 1)
    head = iota((heads, width), 0)
    start = lax.axis_index(TP) * channels
    low = head * HDIM - start
    owned = (lanes >= low) & (lanes < low + HDIM) & (lanes < channels)
    spare = lanes - channels
    listed = (spare == head) | (spare == head + SLOT)
    return jnp.where(owned | listed, 1.0, 0.0).astype(BF16)


def decays(log_ref, doc_ref, picker):
    tokens = log_ref.shape[1]
    mark_column, count_column, count_row = document_counts(doc_ref)
    log_rows = dot(log_ref[...], picker, TN)
    rows, columns = iota((tokens, tokens), 0), iota((tokens, tokens), 1)
    lower = jnp.where(columns <= rows, 1.0, 0.0).astype(BF16)
    cumulative = dot(lower, log_rows.astype(BF16))
    scale = jnp.where(mark_column == 1.0, 1.0, jnp.sqrt(one_minus_exp(2.0 * log_rows)))
    last_count = count_column[tokens - 1 : tokens, :]
    total = cumulative[tokens - 1 : tokens, :]
    centre = cumulative[tokens // 2 : tokens // 2 + 1, :]
    rising = jnp.exp(cumulative - centre)
    falling = jnp.exp(centre - cumulative)
    fresh = jnp.where(count_column == 0.0, 1.0, 0.0)
    inside = jnp.where(count_column == last_count, 1.0, 0.0)
    carry_in = jnp.exp(cumulative) * fresh
    carry_out = jnp.exp(total - cumulative) * inside
    factor = jnp.exp(total) * fresh[tokens - 1 : tokens, :]
    return count_column, count_row, scale, rising, falling, carry_in, carry_out, factor


def two_parts(values):
    high = values.astype(BF16)
    return high, (values - high.astype(F32)).astype(BF16)


def fine_dot(left, right, dims=NN):
    (left_high, left_low), (right_high, right_low) = two_parts(left), two_parts(right)
    small = dot(left_high, right_low, dims) + dot(left_low, right_high, dims)
    return dot(left_high, right_high, dims) + small


class Values(dict):
    __getattr__ = dict.__getitem__


class Staged:
    def __init__(self, ins, outs, through, refs):
        refs = list(refs)
        far_in = [name for name, (_, far) in ins.items() if far is True and name not in through]
        far_out = [name for name, (_, _, far) in outs.items() if far]
        self.refs = {name: refs.pop(0) for name in ins}
        made = {name: refs.pop(0) for name in outs}
        held = {name: refs.pop(0) for name in far_in}
        self.made = Values(made, **{name: refs.pop(0) for name in far_out})
        sems = refs.pop(0) if far_in or far_out or through else None
        self.rest = refs
        self.loads = {
            name: pltpu.make_async_copy(self.refs[name], held[name], sems.at[at])
            for at, name in enumerate(far_in)
        }
        self.stores = {
            name: pltpu.make_async_copy(self.made[name], made[name], sems.at[len(far_in) + at])
            for at, name in enumerate(far_out)
        }
        self.passed = [
            pltpu.make_async_copy(self.refs[name], made[name], sems.at[len(far_in + far_out) + at])
            for at, name in enumerate(through)
        ]
        self.refs.update(held)
        for copy in (*self.loads.values(), *self.passed):
            copy.start()

    def take(self, name):
        if name in self.loads:
            self.loads.pop(name).wait()
        return self.refs[name]

    def __getattr__(self, name):
        return self.take(name)

    def put(self, **values):
        for name, value in values.items():
            self.made[name][...] = value
            self.send(name)

    def send(self, name):
        if name in self.stores:
            self.stores[name].start()

    def finish(self):
        for copy in (*self.stores.values(), *self.passed):
            copy.wait()


def pin(value):
    return pltpu.with_memory_space_constraint(value, pltpu.HBM)


def near(*values):
    return (*values, False)


def far(*values):
    return (*values, True)


def staged_call(body, ins, outs, flops=0, scratch=(), through=()):
    outs = dict(outs, **{name: near(ins[name][0].shape, ins[name][0].dtype) for name in through})

    def kernel(*refs):
        staged = Staged(ins, outs, through, refs)
        body(staged, *staged.rest)
        staged.finish()

    def spec(is_far):
        return pl.BlockSpec(memory_space=pltpu.HBM if is_far else pltpu.VMEM)

    held = [
        pltpu.VMEM(value.shape, value.dtype)
        for name, (value, is_far) in ins.items()
        if is_far is True and name not in through
    ]
    held += [pltpu.VMEM(shape, dtype) for shape, dtype, is_far in outs.values() if is_far]
    copies = len(held) + len(through)
    sems = [pltpu.SemaphoreType.DMA((copies,))] if copies else []
    results = pl.pallas_call(
        kernel,
        name=body.__name__,
        out_shape=[jax.ShapeDtypeStruct(shape, dtype) for shape, dtype, _ in outs.values()],
        in_specs=[spec(is_far) for _, is_far in ins.values()],
        out_specs=[spec(is_far) for _, _, is_far in outs.values()],
        scratch_shapes=held + sems + list(scratch),
        compiler_params=pltpu.CompilerParams(vmem_limit_bytes=24 * 2**20),
        cost_estimate=pl.CostEstimate(flops=flops, bytes_accessed=2**20, transcendentals=0),
    )(*[pin(value) if is_far else value for value, is_far in ins.values()])
    return Values(zip(outs, results))


def assemble(staged, name, whole):
    for step in range(whole.shape[0] // staged.refs[name + "0"].shape[0]):
        block = staged.take(name + "%d" % step)
        piece = block.shape[0]
        start = pl.multiple_of((lax.axis_index(TP) ^ step) * piece, piece)
        whole[pl.ds(start, piece), :] = block[...]


def head_expander(channels, width):
    first = channels // LANE * LANE
    shape = (width - first, width)
    slot = iota(shape, 0) + (first - channels)
    lane = iota(shape, 1)
    spare = lane - channels
    head = jnp.where(slot < SLOT, slot, slot - SLOT)
    low = head * HDIM - lax.axis_index(TP) * channels
    owned = (lane >= low) & (lane < low + HDIM) & (lane < channels)
    listed = (spare == head) | (spare == head + SLOT)
    kept = (slot >= 0) & (slot < 2 * SLOT)
    return jnp.where(kept & (owned | listed), 1.0, 0.0).astype(BF16)


def encode(value, factor, channels):
    lane = iota(value.shape, 1)
    high = factor.astype(BF16).astype(F32)
    listed = jnp.where(lane < channels + SLOT, high, factor - high)
    return jnp.where(lane < channels, value, listed).astype(BF16)


def decode(message, expander):
    return dot(message[:, message.shape[1] - expander.shape[0] :], expander)


def partner_is_later(bit):
    return lax.axis_index(SEQ) % (2 * bit) < bit


def put_message(staged, state_part, grad_part, factor, channels, bit):
    message = staged.made.message
    states = state_part.shape[0]
    if message.shape[0] == states:
        part = jnp.where(partner_is_later(bit), state_part, grad_part)
        message[...] = encode(part, factor, channels)
    else:
        message[:states, :] = encode(state_part, factor, channels)
        message[states:, :] = encode(grad_part, factor, channels)


def prepare(staged):
    tokens, channels = staged.made.enter.shape
    width = staged.made.factor.shape[1]
    log_ref = staged.log
    picker = head_picker(log_ref.shape[0], channels, width)
    count_column, count_row, scale, rising, falling, carry_in, carry_out, factor = decays(
        log_ref, staged.doc, picker
    )
    staged.put(enter=carry_in[:, :channels])
    staged.put(leave=(scale * carry_out)[:, :channels])
    staged.put(rise=rising[:, :channels])
    staged.put(fall=(scale * falling)[:, :channels])
    staged.put(factor=jnp.broadcast_to(factor, staged.made.factor.shape))
    staged.put(expander=head_expander(channels, width))
    rows, columns = iota((tokens, tokens), 0), iota((tokens, tokens), 1)
    same = count_column == count_row
    causal = (rows >= columns) & same
    anticausal = (rows <= columns) & same
    b_rows, c_rows = staged.b_in[...], staged.c_in[...]
    staged.put(causal=jnp.where(causal, 1.0, 0.0))
    staged.put(crossed=jnp.where(causal, dot(c_rows, b_rows, TN), 0.0))
    staged.put(crossed_back=jnp.where(anticausal, dot(b_rows, c_rows, TN), 0.0))
    staged.put(b=b_rows)
    staged.put(c=c_rows)
    staged.put(b_columns=b_rows.astype(F32).T.astype(BF16))
    staged.put(c_columns=c_rows.astype(F32).T.astype(BF16))


def put_summary(staged, name, vectors, values):
    part = staged.made[name]
    part[...] = jnp.zeros_like(part)
    part[:, : values.shape[1]] = dot(staged.take(vectors)[...], values)


def project(staged, rows_ref):
    assemble(staged, "rows", rows_ref)
    rows = rows_ref[...]
    pre = dot(rows, staged.w_in[...], NT)
    staged.put(pre=pre)
    x_rows = (pre * jax.nn.sigmoid(pre)).astype(BF16)
    staged.put(x=x_rows)
    leaving = (x_rows.astype(F32) * staged.leave[...]).astype(BF16)
    staged.put(leaving=leaving)
    put_summary(staged, "state", "b", leaving)
    gate = dot(rows, staged.w_gate[...], NT)
    staged.put(gate=gate)
    staged.put(gated=gate * jax.nn.sigmoid(gate))


def front(staged, grad_ref):
    channels = staged.made.mix.shape[1]
    assemble(staged, "grad", grad_ref)
    mix = dot(grad_ref[...], staged.w_out[...], NT)
    staged.put(mix=mix)
    y_grads = (mix * staged.gated[...]).astype(BF16)
    staged.put(y=y_grads)
    entering = (y_grads.astype(F32) * staged.enter[...]).astype(BF16)
    staged.put(entering=entering)
    put_summary(staged, "grad", "c", entering)
    state_part, grad_part = staged.state[...], staged.made.grad[...]
    put_message(staged, state_part, grad_part, staged.factor[...], channels, 1)


def joined(mine, other, later):
    factor, state, grad = mine
    other_factor, other_state, other_grad = other
    return (
        factor * other_factor,
        jnp.where(later, other_factor * state + other_state, factor * other_state + state),
        jnp.where(later, grad + factor * other_grad, other_grad + other_factor * grad),
    )


def entered(edges, other, later):
    keep, held, back_keep, back_held = edges
    factor, state, grad = other
    return (
        jnp.where(later, keep, keep * factor),
        jnp.where(later, held, keep * state + held),
        jnp.where(later, back_keep * factor, back_keep),
        jnp.where(later, back_keep * grad + back_held, back_held),
    )


def join(channels, bit, flips):
    def join_body(staged):
        expander = staged.expander[...]
        mine = staged.factor[...], staged.state[...], staged.grad[...]
        states = mine[1].shape[0]
        others = []
        for flip in flips:
            received = staged.take("received%d" % flip)
            summaries = received[:states, :].astype(F32), received[states:, :].astype(F32)
            others.append((decode(received[:states, :], expander), *summaries))
        if "keep" in staged.refs:
            refs = staged.keep, staged.held, staged.back_keep, staged.back_held
            edges = tuple(ref[...] for ref in refs)
        else:
            one, none = jnp.ones_like(mine[0]), jnp.zeros_like(mine[0])
            edges = one, none, one, none
        later = partner_is_later(bit)
        edges, mine = entered(edges, others[0], later), joined(mine, others[0], later)
        if len(flips) == 3:
            pair, later = joined(others[1], others[2], later), partner_is_later(2 * bit)
            edges, mine = entered(edges, pair, later), joined(mine, pair, later)
        staged.put(keep=edges[0], held=edges[1], back_keep=edges[2], back_held=edges[3])
        factor, state, grad = mine
        put_message(staged, state, grad, factor, channels, bit * (len(flips) + 1))
        if "state" in staged.made:
            staged.put(state=state, grad=grad, factor=factor)

    return join_body


def slopes(staged):
    staged.put(pre_slope=silu_slope(staged.pre[...]))
    staged.put(gate_slope=staged.mix[...] * silu_slope(staged.gate[...]))


def local_vectors(staged):
    upper = staged.y[...].astype(F32) * staged.rise[...]
    lower = staged.x[...].astype(F32) * staged.fall[...]
    causal = staged.causal[...] > 0.0
    high, low = two_parts(jnp.where(causal, fine_dot(upper, lower, NT), 0.0))
    b_rows, c_rows = staged.b[...], staged.c[...]
    states = b_rows.shape[0]
    bc = staged.made.bc
    bc[:states, :] = dot(c_rows, high) + dot(c_rows, low)
    bc[states:, :] = dot(b_rows, high, NT) + dot(b_rows, low, NT)


def local_channels(staged):
    x_rows, y_grads = staged.x[...].astype(F32), staged.y[...].astype(F32)
    rise, fall, skip = staged.rise[...], staged.fall[...], staged.skip[...]
    ssm = rise * fine_dot(staged.crossed[...], x_rows * fall)
    staged.put(ssm=ssm + skip * x_rows)
    x_grad = fall * fine_dot(staged.crossed_back[...], y_grads * rise)
    staged.put(x_grad=x_grad + skip * y_grads)


def put_pieces(staged, steps, state_in, grad_in, bc, gate_ref, pre_ref):
    tp = lax.axis_index(TP)
    tokens = gate_ref.shape[0]
    piece = tokens // len(steps)
    half = pl.ds(pl.multiple_of((tp ^ steps[0]) // 2 * tokens, tokens), tokens)
    carried = dot(staged.c_columns[half, :], state_in)
    ssm_out = staged.ssm[half, :] + staged.enter[half, :] * carried
    gate_ref[...] = (ssm_out.astype(BF16).astype(F32) * staged.gate_slope[half, :]).astype(BF16)
    carried = dot(staged.b_columns[half, :], grad_in)
    x_grad = staged.x_grad[half, :] + staged.leave[half, :] * carried
    pre_ref[...] = (x_grad.astype(BF16).astype(F32) * staged.pre_slope[half, :]).astype(BF16)
    starts = [pl.multiple_of((tp ^ step) % 2 * piece, piece) for step in steps]
    gate_rows, pre_rows = (
        jnp.concatenate([ref[pl.ds(start, piece), :] for start in starts], axis=0)
        for ref in (gate_ref, pre_ref)
    )
    partial = dot(gate_rows, staged.w_gate[...]) + dot(pre_rows, staged.w_in[...])
    depth = partial.shape[1]
    for at, step in enumerate(steps):
        made = staged.made["part%d" % step]
        split = made.shape[1] - bc.shape[1]
        if split > depth:
            made[:, split - LANE : split] = jnp.zeros((piece, LANE), made.dtype)
        made[:, :depth] = partial[at * piece : (at + 1) * piece, :].astype(made.dtype)
        made[: bc.shape[0], split:] = bc.astype(made.dtype)


def back(bit, steps):
    def back_body(staged, gate_ref, pre_ref):
        entry = staged.entry[...]
        states, channels = entry.shape
        received = staged.received
        other_part = received[:, :channels].astype(F32)
        other = decode(received[...], staged.expander[...])[:, :channels]
        later = partner_is_later(bit)
        keep, held, back_keep, back_held = (
            ref[:, :channels]
            for ref in (staged.keep, staged.held, staged.back_keep, staged.back_held)
        )
        state = jnp.where(later, entry, other * entry + other_part)
        state_in = (keep * state + held).astype(BF16)
        grad_in = jnp.where(later, back_keep * other_part + back_held, back_held).astype(BF16)
        staged.put(state_in=state_in, grad_in=grad_in)
        bc = staged.made.bc
        local = staged.bc
        bc[:states, :] = local[:states, :] + dot(grad_in, staged.leaving[...], NT)
        bc[states:, :] = local[states:, :] + dot(state_in, staged.entering[...], NT)
        put_pieces(staged, steps, state_in, grad_in, bc[...], gate_ref, pre_ref)

    return back_body


def rest(steps):
    def rest_body(staged, gate_ref, pre_ref):
        state_in, grad_in = staged.state_in[...], staged.grad_in[...]
        put_pieces(staged, steps, state_in, grad_in, staged.bc[...], gate_ref, pre_ref)

    return rest_body


def add(staged):
    values = [staged.take(name)[...].astype(F32) for name in staged.refs]
    staged.put(sum=sum(values).astype(staged.made.sum.dtype))


def total(staged):
    depth = staged.made.grad.shape[1]
    states, tokens = staged.made.b.shape
    received = [staged.take(name) for name in staged.refs]
    split = received[0].shape[1] - tokens
    staged.put(grad=sum(part[:, :depth].astype(F32) for part in received).astype(BF16))
    staged.put(b=sum(part[:states, split:].astype(F32) for part in received))
    staged.put(c=sum(part[states : 2 * states, split:].astype(F32) for part in received))


def swap_masks(parts):
    masks, bit = [], parts // 2
    while bit:
        masks.append(bit)
        bit //= 2
    return masks


def shards(
    layer_input, out_grad, w_in, w_gate, w_out, b_proj, c_proj, log_decay, d_skip, entry_state,
    doc_start,
):
    owners, parts = lax.axis_size(SEQ), lax.axis_size(TP)
    assert owners > 2 and owners & (owners - 1) == 0 and parts == 4
    piece, depth = layer_input.shape
    tokens = piece * parts
    channels = w_in.shape[0]
    states = b_proj.shape[0]
    width = round_up(channels + 2 * SLOT, LANE)
    wide = near((tokens, channels), F32)
    half = near((tokens, channels), BF16)
    square = near((tokens, tokens), F32)
    row = near((states, tokens), BF16)
    column = near((tokens, states), BF16)
    summary = near((states, width), F32)

    def ordered(value, after):
        return lax.optimization_barrier((value, after))[0]

    def swap(value, axis, bit):
        size = lax.axis_size(axis)
        return lax.ppermute(value, axis, [(at, at ^ bit) for at in range(size)])

    def call(body, ins, outs, **options):
        ins = {key: near(value) if hasattr(value, "shape") else value for key, value in ins.items()}
        return staged_call(body, ins, outs, **options)

    far_ins = dict(
        log=log_decay, doc=doc_start.reshape(1, tokens), b_in=b_proj, c_in=c_proj, w_gate=w_gate,
        w_in=w_in, w_out=w_out, rows0=layer_input, grad0=out_grad, entry=entry_state,
        skip=d_skip.reshape(1, channels),
    )
    ready = call(
        prepare, {name: far(value) for name, value in far_ins.items()},
        dict(enter=wide, leave=wide, rise=wide, fall=wide, factor=summary,
             expander=near((width - channels // LANE * LANE, width), BF16), causal=square,
             crossed=square, crossed_back=square, b=row, c=row, b_columns=column, c_columns=column),
        flops=8 * tokens * channels * tokens,
        through=("w_gate", "w_in", "w_out", "rows0", "grad0", "entry", "skip"),
    )
    grad_blocks, row_blocks = {0: out_grad}, {0: layer_input}
    masks = swap_masks(parts)
    for mask in masks:
        for blocks in (row_blocks, grad_blocks):
            for step in list(blocks):
                block = blocks[step]
                if mask != masks[0]:
                    block = ordered(block, ready.expander)
                blocks[step ^ mask] = swap(block, TP, mask)
    rows = {"rows%d" % step: block for step, block in row_blocks.items()}
    grads = {"grad%d" % step: block for step, block in grad_blocks.items()}
    rows["rows0"], grads["grad0"] = ready.rows0, ready.grad0
    assembled = pltpu.VMEM((tokens, depth), BF16)
    both = near((2 * states, width), BF16)
    one = near((states, width), BF16)
    first = call(
        project,
        dict(rows, **dict(w_gate=ready.w_gate, w_in=ready.w_in, b=ready.b, leave=ready.leave)),
        dict(gate=wide, gated=wide, pre=wide, x=half, leaving=half, state=summary),
        flops=4 * tokens * channels * depth, scratch=(assembled,),
    )
    first.update(call(
        front,
        dict(grads, **dict(w_out=ready.w_out, c=ready.c, enter=ready.enter, factor=ready.factor),
             **dict(gated=first.gated, state=first.state)),
        dict(mix=wide, y=half, entering=half, grad=summary, message=both),
        flops=2 * tokens * channels * depth, scratch=(assembled,),
    ))
    group = dict(state=first.state, grad=first.grad, factor=ready.factor)
    message, x_rows, y_grads = first.message, first.x, first.y
    results, bit = {}, 1
    while 2 * bit < owners:
        flips = (bit, 2 * bit, 3 * bit) if 4 * bit < owners else (bit,)
        arrived = {flip: swap(message, SEQ, flip) for flip in flips}
        if bit == 1:
            slope = call(
                slopes, dict(pre=first.pre, gate=first.gate, mix=first.mix),
                dict(pre_slope=wide, gate_slope=wide), flops=tokens * channels * 32,
            )
            results.update(call(
                local_vectors,
                dict(rise=ready.rise, fall=ready.fall, causal=ready.causal, b=ready.b, c=ready.c,
                     x=x_rows, y=ordered(y_grads, slope.pre_slope)),
                dict(bc=near((2 * states, tokens), F32)), flops=8 * tokens * channels * tokens,
            ))
            arrived[flips[-1]] = ordered(arrived[flips[-1]], results["bc"])
        after = bit * (len(flips) + 1)
        last = 2 * after >= owners
        outs = dict(keep=summary, held=summary, back_keep=summary, back_held=summary,
                    message=one if last else both)
        if not last:
            outs.update(state=summary, grad=summary, factor=summary)
        group = call(
            join(channels, bit, flips),
            dict(group, expander=ready.expander,
                 **{"received%d" % flip: value for flip, value in arrived.items()}),
            outs,
        )
        message = group.pop("message")
        bit = after
    received = swap(message, SEQ, bit)
    results.update(call(
        local_channels,
        dict(rise=ready.rise, fall=ready.fall, crossed=ready.crossed,
             crossed_back=ready.crossed_back, skip=ready.skip,
             x=ordered(x_rows, group.keep), y=y_grads),
        dict(ssm=wide, x_grad=wide), flops=16 * tokens * channels * tokens,
    ))
    span = round_up(depth, LANE) + tokens
    graded = pltpu.VMEM((tokens // 2, channels), BF16)
    kept, urgent, others = (0, 2), (2, 3), (0, 1)

    def named(steps):
        types = {step: F32 if step in kept else BF16 for step in steps}
        return {"part%d" % step: near((piece, span), types[step]) for step in steps}

    entered = near((states, channels), BF16)
    shared = dict(
        results, pre_slope=slope.pre_slope, gate_slope=slope.gate_slope, enter=ready.enter,
        leave=ready.leave, b_columns=ready.b_columns, c_columns=ready.c_columns,
        w_gate=ready.w_gate, w_in=ready.w_in,
    )
    held = call(
        back(bit, urgent),
        dict(shared, **group, received=received, entering=first.entering, leaving=first.leaving,
             entry=ready.entry, expander=ready.expander),
        dict(named(urgent), bc=near((2 * states, tokens), F32), state_in=entered, grad_in=entered),
        flops=2 * tokens * channels * depth, scratch=(graded, graded),
    )

    def added(dtype, one, two, **options):
        return call(add, dict(one=one, two=two), dict(sum=near((piece, span), dtype)), **options).sum

    far_sum = added(BF16, held.part2, swap(held.part3, TP, 1))
    distant = swap(far_sum, TP, 2)
    shared.update(
        bc=held.bc, state_in=ordered(held.state_in, far_sum), grad_in=held.grad_in
    )
    held.update(call(
        rest(others), shared, named(others),
        flops=2 * tokens * channels * depth, scratch=(graded, graded),
    ))
    own = added(F32, held.part0, distant, flops=tokens * channels * depth)
    result = call(
        total, dict(own=own, across=swap(held.part1, TP, 1)),
        dict(grad=near((piece, depth), BF16), b=near((states, tokens), F32),
             c=near((states, tokens), F32)),
    )
    return result.grad, result.b, result.c


def solution(mesh):
    in_specs = (
        P((SEQ, TP), None),
        P((SEQ, TP), None),
        P(TP, None),
        P(TP, None),
        P(TP, None),
        P(None, SEQ),
        P(None, SEQ),
        P(None, SEQ),
        P(TP),
        P(None, TP),
        P(SEQ),
    )
    out_specs = (P((SEQ, TP), None), P(None, SEQ), P(None, SEQ))
    return jax.shard_map(shards, mesh=mesh, in_specs=in_specs, out_specs=out_specs, check_vma=False)
```

```python
import jax
import jax.numpy as jnp
from jax import lax
from jax.experimental import pallas as pl
from jax.experimental.pallas import tpu as pltpu
from jax.sharding import PartitionSpec as P

HDIM = 64
LANE = 128
SLOT = 32
SEQ, TP = "seq", "tp"

F32 = jnp.float32
BF16 = jnp.bfloat16
NN = (((1,), (0,)), ((), ()))
NT = (((1,), (1,)), ((), ()))
TN = (((0,), (0,)), ((), ()))


def dot(left, right, dims=NN):
    return lax.dot_general(left, right, dims, preferred_element_type=F32)


def round_up(value, step):
    return -(-value // step) * step


def silu_slope(values):
    logistic = jax.nn.sigmoid(values)
    return logistic * (1.0 + values * (1.0 - logistic))


def iota(shape, axis):
    return lax.broadcasted_iota(jnp.int32, shape, axis)


def one_minus_exp(values):
    series = 1.0 + values * (1.0 / 7.0)
    for term in (6.0, 5.0, 4.0, 3.0, 2.0):
        series = 1.0 + values * (1.0 / term) * series
    return jnp.where(values > -0.35, -values * series, 1.0 - jnp.exp(values))


def document_counts(doc_ref):
    tokens = doc_ref.shape[1]
    rows, columns = iota((tokens, tokens), 0), iota((tokens, tokens), 1)
    first = (iota((1, tokens), 1) == 0) & (lax.axis_index(SEQ) == 0)
    mark_row = jnp.where(first, 0.0, doc_ref[...].astype(F32))
    mark_row = jnp.broadcast_to(mark_row, (tokens, tokens))
    mark_column = jnp.sum(jnp.where(rows == columns, mark_row, 0.0), axis=1, keepdims=True)
    count_column = jnp.sum(jnp.where(columns <= rows, mark_row, 0.0), axis=1, keepdims=True)
    count_row = jnp.sum(
        jnp.where(rows <= columns, jnp.broadcast_to(mark_column, (tokens, tokens)), 0.0),
        axis=0,
        keepdims=True,
    )
    return mark_column, count_column, count_row


def head_picker(heads, channels, width):
    lanes = iota((heads, width), 1)
    head = iota((heads, width), 0)
    start = lax.axis_index(TP) * channels
    low = head * HDIM - start
    owned = (lanes >= low) & (lanes < low + HDIM) & (lanes < channels)
    spare = lanes - channels
    listed = (spare == head) | (spare == head + SLOT)
    return jnp.where(owned | listed, 1.0, 0.0).astype(BF16)


def decays(log_ref, doc_ref, picker):
    tokens = log_ref.shape[1]
    mark_column, count_column, count_row = document_counts(doc_ref)
    log_rows = dot(log_ref[...], picker, TN)
    rows, columns = iota((tokens, tokens), 0), iota((tokens, tokens), 1)
    lower = jnp.where(columns <= rows, 1.0, 0.0).astype(BF16)
    cumulative = dot(lower, log_rows.astype(BF16))
    scale = jnp.where(mark_column == 1.0, 1.0, jnp.sqrt(one_minus_exp(2.0 * log_rows)))
    last_count = count_column[tokens - 1 : tokens, :]
    total = cumulative[tokens - 1 : tokens, :]
    centre = cumulative[tokens // 2 : tokens // 2 + 1, :]
    rising = jnp.exp(cumulative - centre)
    falling = jnp.exp(centre - cumulative)
    fresh = jnp.where(count_column == 0.0, 1.0, 0.0)
    inside = jnp.where(count_column == last_count, 1.0, 0.0)
    carry_in = jnp.exp(cumulative) * fresh
    carry_out = jnp.exp(total - cumulative) * inside
    factor = jnp.exp(total) * fresh[tokens - 1 : tokens, :]
    return count_column, count_row, scale, rising, falling, carry_in, carry_out, factor


def two_parts(values):
    high = values.astype(BF16)
    return high, (values - high.astype(F32)).astype(BF16)


def fine_dot(left, right, dims=NN):
    (left_high, left_low), (right_high, right_low) = two_parts(left), two_parts(right)
    small = dot(left_high, right_low, dims) + dot(left_low, right_high, dims)
    return dot(left_high, right_high, dims) + small


class Values(dict):
    __getattr__ = dict.__getitem__


class Staged:
    def __init__(self, ins, outs, through, refs):
        refs = list(refs)
        far_in = [name for name, (_, far) in ins.items() if far is True and name not in through]
        far_out = [name for name, (_, _, far) in outs.items() if far]
        self.refs = {name: refs.pop(0) for name in ins}
        made = {name: refs.pop(0) for name in outs}
        held = {name: refs.pop(0) for name in far_in}
        self.made = Values(made, **{name: refs.pop(0) for name in far_out})
        sems = refs.pop(0) if far_in or far_out or through else None
        self.rest = refs
        self.loads = {
            name: pltpu.make_async_copy(self.refs[name], held[name], sems.at[at])
            for at, name in enumerate(far_in)
        }
        self.stores = {
            name: pltpu.make_async_copy(self.made[name], made[name], sems.at[len(far_in) + at])
            for at, name in enumerate(far_out)
        }
        self.passed = [
            pltpu.make_async_copy(self.refs[name], made[name], sems.at[len(far_in + far_out) + at])
            for at, name in enumerate(through)
        ]
        self.refs.update(held)
        for copy in (*self.loads.values(), *self.passed):
            copy.start()

    def take(self, name):
        if name in self.loads:
            self.loads.pop(name).wait()
        return self.refs[name]

    def __getattr__(self, name):
        return self.take(name)

    def put(self, **values):
        for name, value in values.items():
            self.made[name][...] = value
            self.send(name)

    def send(self, name):
        if name in self.stores:
            self.stores[name].start()

    def finish(self):
        for copy in (*self.stores.values(), *self.passed):
            copy.wait()


def pin(value):
    return pltpu.with_memory_space_constraint(value, pltpu.HBM)


def near(*values):
    return (*values, False)


def far(*values):
    return (*values, True)


def staged_call(body, ins, outs, flops=0, scratch=(), through=()):
    outs = dict(outs, **{name: near(ins[name][0].shape, ins[name][0].dtype) for name in through})

    def kernel(*refs):
        staged = Staged(ins, outs, through, refs)
        body(staged, *staged.rest)
        staged.finish()

    def spec(is_far):
        return pl.BlockSpec(memory_space=pltpu.HBM if is_far else pltpu.VMEM)

    held = [
        pltpu.VMEM(value.shape, value.dtype)
        for name, (value, is_far) in ins.items()
        if is_far is True and name not in through
    ]
    held += [pltpu.VMEM(shape, dtype) for shape, dtype, is_far in outs.values() if is_far]
    copies = len(held) + len(through)
    sems = [pltpu.SemaphoreType.DMA((copies,))] if copies else []
    results = pl.pallas_call(
        kernel,
        name=body.__name__,
        out_shape=[jax.ShapeDtypeStruct(shape, dtype) for shape, dtype, _ in outs.values()],
        in_specs=[spec(is_far) for _, is_far in ins.values()],
        out_specs=[spec(is_far) for _, _, is_far in outs.values()],
        scratch_shapes=held + sems + list(scratch),
        compiler_params=pltpu.CompilerParams(vmem_limit_bytes=24 * 2**20),
        cost_estimate=pl.CostEstimate(flops=flops, bytes_accessed=2**20, transcendentals=0),
    )(*[pin(value) if is_far else value for value, is_far in ins.values()])
    return Values(zip(outs, results))


def assemble(staged, name, whole):
    for step in range(whole.shape[0] // staged.refs[name + "0"].shape[0]):
        block = staged.take(name + "%d" % step)
        piece = block.shape[0]
        start = pl.multiple_of((lax.axis_index(TP) ^ step) * piece, piece)
        whole[pl.ds(start, piece), :] = block[...]


def head_expander(channels, width):
    first = channels // LANE * LANE
    shape = (width - first, width)
    slot = iota(shape, 0) + (first - channels)
    lane = iota(shape, 1)
    spare = lane - channels
    head = jnp.where(slot < SLOT, slot, slot - SLOT)
    low = head * HDIM - lax.axis_index(TP) * channels
    owned = (lane >= low) & (lane < low + HDIM) & (lane < channels)
    listed = (spare == head) | (spare == head + SLOT)
    kept = (slot >= 0) & (slot < 2 * SLOT)
    return jnp.where(kept & (owned | listed), 1.0, 0.0).astype(BF16)


def encode(value, factor, channels):
    lane = iota(value.shape, 1)
    high = factor.astype(BF16).astype(F32)
    listed = jnp.where(lane < channels + SLOT, high, factor - high)
    return jnp.where(lane < channels, value, listed).astype(BF16)


def decode(message, expander):
    return dot(message[:, message.shape[1] - expander.shape[0] :], expander)


def partner_is_later(bit):
    return lax.axis_index(SEQ) % (2 * bit) < bit


def put_message(staged, state_part, grad_part, factor, channels, bit):
    message = staged.made.message
    states = state_part.shape[0]
    if message.shape[0] == states:
        part = jnp.where(partner_is_later(bit), state_part, grad_part)
        message[...] = encode(part, factor, channels)
    else:
        message[:states, :] = encode(state_part, factor, channels)
        message[states:, :] = encode(grad_part, factor, channels)


def prepare(staged):
    tokens, channels = staged.made.enter.shape
    width = staged.made.factor.shape[1]
    log_ref = staged.log
    picker = head_picker(log_ref.shape[0], channels, width)
    count_column, count_row, scale, rising, falling, carry_in, carry_out, factor = decays(
        log_ref, staged.doc, picker
    )
    staged.put(enter=carry_in[:, :channels])
    staged.put(leave=(scale * carry_out)[:, :channels])
    staged.put(rise=rising[:, :channels])
    staged.put(fall=(scale * falling)[:, :channels])
    staged.put(factor=jnp.broadcast_to(factor, staged.made.factor.shape))
    staged.put(expander=head_expander(channels, width))
    rows, columns = iota((tokens, tokens), 0), iota((tokens, tokens), 1)
    same = count_column == count_row
    causal = (rows >= columns) & same
    anticausal = (rows <= columns) & same
    b_rows, c_rows = staged.b_in[...], staged.c_in[...]
    staged.put(causal=jnp.where(causal, 1.0, 0.0))
    staged.put(crossed=jnp.where(causal, dot(c_rows, b_rows, TN), 0.0))
    staged.put(crossed_back=jnp.where(anticausal, dot(b_rows, c_rows, TN), 0.0))
    staged.put(b=b_rows)
    staged.put(c=c_rows)
    staged.put(b_columns=b_rows.astype(F32).T.astype(BF16))
    staged.put(c_columns=c_rows.astype(F32).T.astype(BF16))


def put_summary(staged, name, vectors, values):
    part = staged.made[name]
    part[...] = jnp.zeros_like(part)
    part[:, : values.shape[1]] = dot(staged.take(vectors)[...], values)


def project(staged, rows_ref):
    assemble(staged, "rows", rows_ref)
    rows = rows_ref[...]
    pre = dot(rows, staged.w_in[...], NT)
    staged.put(pre=pre)
    x_rows = (pre * jax.nn.sigmoid(pre)).astype(BF16)
    staged.put(x=x_rows)
    leaving = (x_rows.astype(F32) * staged.leave[...]).astype(BF16)
    staged.put(leaving=leaving)
    put_summary(staged, "state", "b", leaving)
    gate = dot(rows, staged.w_gate[...], NT)
    staged.put(gate=gate)
    staged.put(gated=gate * jax.nn.sigmoid(gate))


def front(staged, grad_ref):
    channels = staged.made.mix.shape[1]
    assemble(staged, "grad", grad_ref)
    mix = dot(grad_ref[...], staged.w_out[...], NT)
    staged.put(mix=mix)
    y_grads = (mix * staged.gated[...]).astype(BF16)
    staged.put(y=y_grads)
    entering = (y_grads.astype(F32) * staged.enter[...]).astype(BF16)
    staged.put(entering=entering)
    put_summary(staged, "grad", "c", entering)
    state_part, grad_part = staged.state[...], staged.made.grad[...]
    put_message(staged, state_part, grad_part, staged.factor[...], channels, 1)


def joined(mine, other, later):
    factor, state, grad = mine
    other_factor, other_state, other_grad = other
    return (
        factor * other_factor,
        jnp.where(later, other_factor * state + other_state, factor * other_state + state),
        jnp.where(later, grad + factor * other_grad, other_grad + other_factor * grad),
    )


def entered(edges, other, later):
    keep, held, back_keep, back_held = edges
    factor, state, grad = other
    return (
        jnp.where(later, keep, keep * factor),
        jnp.where(later, held, keep * state + held),
        jnp.where(later, back_keep * factor, back_keep),
        jnp.where(later, back_keep * grad + back_held, back_held),
    )


def join(channels, bit, flips):
    def join_body(staged):
        expander = staged.expander[...]
        mine = staged.factor[...], staged.state[...], staged.grad[...]
        states = mine[1].shape[0]
        others = []
        for flip in flips:
            received = staged.take("received%d" % flip)
            summaries = received[:states, :].astype(F32), received[states:, :].astype(F32)
            others.append((decode(received[:states, :], expander), *summaries))
        if "keep" in staged.refs:
            refs = staged.keep, staged.held, staged.back_keep, staged.back_held
            edges = tuple(ref[...] for ref in refs)
        else:
            one, none = jnp.ones_like(mine[0]), jnp.zeros_like(mine[0])
            edges = one, none, one, none
        later = partner_is_later(bit)
        edges, mine = entered(edges, others[0], later), joined(mine, others[0], later)
        if len(flips) == 3:
            pair, later = joined(others[1], others[2], later), partner_is_later(2 * bit)
            edges, mine = entered(edges, pair, later), joined(mine, pair, later)
        staged.put(keep=edges[0], held=edges[1], back_keep=edges[2], back_held=edges[3])
        factor, state, grad = mine
        put_message(staged, state, grad, factor, channels, bit * (len(flips) + 1))
        if "state" in staged.made:
            staged.put(state=state, grad=grad, factor=factor)

    return join_body


def slopes(staged):
    staged.put(pre_slope=silu_slope(staged.pre[...]))
    staged.put(gate_slope=staged.mix[...] * silu_slope(staged.gate[...]))


def local_vectors(staged):
    upper = staged.y[...].astype(F32) * staged.rise[...]
    lower = staged.x[...].astype(F32) * staged.fall[...]
    causal = staged.causal[...] > 0.0
    high, low = two_parts(jnp.where(causal, fine_dot(upper, lower, NT), 0.0))
    b_rows, c_rows = staged.b[...], staged.c[...]
    states = b_rows.shape[0]
    bc = staged.made.bc
    bc[:states, :] = dot(c_rows, high) + dot(c_rows, low)
    bc[states:, :] = dot(b_rows, high, NT) + dot(b_rows, low, NT)


def local_channels(staged):
    x_rows, y_grads = staged.x[...].astype(F32), staged.y[...].astype(F32)
    rise, fall, skip = staged.rise[...], staged.fall[...], staged.skip[...]
    ssm = rise * fine_dot(staged.crossed[...], x_rows * fall)
    staged.put(ssm=ssm + skip * x_rows)
    x_grad = fall * fine_dot(staged.crossed_back[...], y_grads * rise)
    staged.put(x_grad=x_grad + skip * y_grads)


def put_pieces(staged, steps, state_in, grad_in, bc, gate_ref, pre_ref):
    tp = lax.axis_index(TP)
    tokens = gate_ref.shape[0]
    piece = tokens // len(steps)
    half = pl.ds(pl.multiple_of((tp ^ steps[0]) // 2 * tokens, tokens), tokens)
    carried = dot(staged.c_columns[half, :], state_in)
    ssm_out = staged.ssm[half, :] + staged.enter[half, :] * carried
    gate_ref[...] = (ssm_out.astype(BF16).astype(F32) * staged.gate_slope[half, :]).astype(BF16)
    carried = dot(staged.b_columns[half, :], grad_in)
    x_grad = staged.x_grad[half, :] + staged.leave[half, :] * carried
    pre_ref[...] = (x_grad.astype(BF16).astype(F32) * staged.pre_slope[half, :]).astype(BF16)
    starts = [pl.multiple_of((tp ^ step) % 2 * piece, piece) for step in steps]
    gate_rows, pre_rows = (
        jnp.concatenate([ref[pl.ds(start, piece), :] for start in starts], axis=0)
        for ref in (gate_ref, pre_ref)
    )
    partial = dot(gate_rows, staged.w_gate[...]) + dot(pre_rows, staged.w_in[...])
    depth = partial.shape[1]
    for at, step in enumerate(steps):
        made = staged.made["part%d" % step]
        split = made.shape[1] - bc.shape[1]
        if split > depth:
            made[:, split - LANE : split] = jnp.zeros((piece, LANE), made.dtype)
        made[:, :depth] = partial[at * piece : (at + 1) * piece, :].astype(made.dtype)
        made[: bc.shape[0], split:] = bc.astype(made.dtype)


def back(bit, steps):
    def back_body(staged, gate_ref, pre_ref):
        entry = staged.entry[...]
        states, channels = entry.shape
        received = staged.received
        other_part = received[:, :channels].astype(F32)
        other = decode(received[...], staged.expander[...])[:, :channels]
        later = partner_is_later(bit)
        keep, held, back_keep, back_held = (
            ref[:, :channels]
            for ref in (staged.keep, staged.held, staged.back_keep, staged.back_held)
        )
        state = jnp.where(later, entry, other * entry + other_part)
        state_in = (keep * state + held).astype(BF16)
        grad_in = jnp.where(later, back_keep * other_part + back_held, back_held).astype(BF16)
        staged.put(state_in=state_in, grad_in=grad_in)
        bc = staged.made.bc
        local = staged.bc
        bc[:states, :] = local[:states, :] + dot(grad_in, staged.leaving[...], NT)
        bc[states:, :] = local[states:, :] + dot(state_in, staged.entering[...], NT)
        put_pieces(staged, steps, state_in, grad_in, bc[...], gate_ref, pre_ref)

    return back_body


def rest(steps):
    def rest_body(staged, gate_ref, pre_ref):
        state_in, grad_in = staged.state_in[...], staged.grad_in[...]
        put_pieces(staged, steps, state_in, grad_in, staged.bc[...], gate_ref, pre_ref)

    return rest_body


def add(staged):
    values = [staged.take(name)[...].astype(F32) for name in staged.refs]
    staged.put(sum=sum(values).astype(staged.made.sum.dtype))


def total(staged):
    depth = staged.made.grad.shape[1]
    states, tokens = staged.made.b.shape
    received = [staged.take(name) for name in staged.refs]
    split = received[0].shape[1] - tokens
    staged.put(grad=sum(part[:, :depth].astype(F32) for part in received).astype(BF16))
    staged.put(b=sum(part[:states, split:].astype(F32) for part in received))
    staged.put(c=sum(part[states : 2 * states, split:].astype(F32) for part in received))


def swap_masks(parts):
    masks, bit = [], parts // 2
    while bit:
        masks.append(bit)
        bit //= 2
    return masks


def shards(
    layer_input, out_grad, w_in, w_gate, w_out, b_proj, c_proj, log_decay, d_skip, entry_state,
    doc_start,
):
    owners, parts = lax.axis_size(SEQ), lax.axis_size(TP)
    assert owners > 2 and owners & (owners - 1) == 0 and parts == 4
    piece, depth = layer_input.shape
    tokens = piece * parts
    channels = w_in.shape[0]
    states = b_proj.shape[0]
    width = round_up(channels + 2 * SLOT, LANE)
    wide = near((tokens, channels), F32)
    half = near((tokens, channels), BF16)
    square = near((tokens, tokens), F32)
    row = near((states, tokens), BF16)
    column = near((tokens, states), BF16)
    summary = near((states, width), F32)

    def ordered(value, after):
        return lax.optimization_barrier((value, after))[0]

    def swap(value, axis, bit):
        size = lax.axis_size(axis)
        return lax.ppermute(value, axis, [(at, at ^ bit) for at in range(size)])

    def call(body, ins, outs, **options):
        ins = {key: near(value) if hasattr(value, "shape") else value for key, value in ins.items()}
        return staged_call(body, ins, outs, **options)

    far_ins = dict(
        doc=doc_start.reshape(1, tokens), b_in=b_proj, c_in=c_proj, w_gate=w_gate,
        w_in=w_in, w_out=w_out, rows0=layer_input, grad0=out_grad, entry=entry_state,
        skip=d_skip.reshape(1, channels),
    )
    ready = call(
        prepare, dict(log=log_decay, **{name: far(value) for name, value in far_ins.items()}),
        dict(enter=wide, leave=wide, rise=wide, fall=wide, factor=summary,
             expander=near((width - channels // LANE * LANE, width), BF16), causal=square,
             crossed=square, crossed_back=square, b=row, c=row, b_columns=column, c_columns=column),
        flops=8 * tokens * channels * tokens,
        through=("w_gate", "w_in", "w_out", "rows0", "grad0", "entry", "skip"),
    )
    grad_blocks, row_blocks = {0: out_grad}, {0: layer_input}
    masks = swap_masks(parts)
    for mask in masks:
        for blocks in (row_blocks, grad_blocks):
            for step in list(blocks):
                block = blocks[step]
                if mask != masks[0]:
                    block = ordered(block, ready.expander)
                blocks[step ^ mask] = swap(block, TP, mask)
    rows = {"rows%d" % step: block for step, block in row_blocks.items()}
    grads = {"grad%d" % step: block for step, block in grad_blocks.items()}
    rows["rows0"], grads["grad0"] = ready.rows0, ready.grad0
    assembled = pltpu.VMEM((tokens, depth), BF16)
    both = near((2 * states, width), BF16)
    one = near((states, width), BF16)
    first = call(
        project,
        dict(rows, **dict(w_gate=ready.w_gate, w_in=ready.w_in, b=ready.b, leave=ready.leave)),
        dict(gate=wide, gated=wide, pre=wide, x=half, leaving=half, state=summary),
        flops=4 * tokens * channels * depth, scratch=(assembled,),
    )
    first.update(call(
        front,
        dict(grads, **dict(w_out=ready.w_out, c=ready.c, enter=ready.enter, factor=ready.factor),
             **dict(gated=first.gated, state=first.state)),
        dict(mix=wide, y=half, entering=half, grad=summary, message=both),
        flops=2 * tokens * channels * depth, scratch=(assembled,),
    ))
    group = dict(state=first.state, grad=first.grad, factor=ready.factor)
    message, x_rows, y_grads = first.message, first.x, first.y
    results, bit = {}, 1
    while 2 * bit < owners:
        flips = (bit, 2 * bit, 3 * bit) if 4 * bit < owners else (bit,)
        arrived = {flip: swap(message, SEQ, flip) for flip in flips}
        if bit == 1:
            slope = call(
                slopes, dict(pre=first.pre, gate=first.gate, mix=first.mix),
                dict(pre_slope=wide, gate_slope=wide), flops=tokens * channels * 32,
            )
            results.update(call(
                local_vectors,
                dict(rise=ready.rise, fall=ready.fall, causal=ready.causal, b=ready.b, c=ready.c,
                     x=x_rows, y=ordered(y_grads, slope.pre_slope)),
                dict(bc=near((2 * states, tokens), F32)), flops=8 * tokens * channels * tokens,
            ))
            arrived[flips[-1]] = ordered(arrived[flips[-1]], results["bc"])
        after = bit * (len(flips) + 1)
        last = 2 * after >= owners
        outs = dict(keep=summary, held=summary, back_keep=summary, back_held=summary,
                    message=one if last else both)
        if not last:
            outs.update(state=summary, grad=summary, factor=summary)
        group = call(
            join(channels, bit, flips),
            dict(group, expander=ready.expander,
                 **{"received%d" % flip: value for flip, value in arrived.items()}),
            outs,
        )
        message = group.pop("message")
        bit = after
    received = swap(message, SEQ, bit)
    results.update(call(
        local_channels,
        dict(rise=ready.rise, fall=ready.fall, crossed=ready.crossed,
             crossed_back=ready.crossed_back, skip=ready.skip,
             x=ordered(x_rows, group.keep), y=y_grads),
        dict(ssm=wide, x_grad=wide), flops=16 * tokens * channels * tokens,
    ))
    span = round_up(depth, LANE) + tokens
    graded = pltpu.VMEM((tokens // 2, channels), BF16)
    kept, urgent, others = (0, 2), (2, 3), (0, 1)

    def named(steps):
        types = {step: F32 if step in kept else BF16 for step in steps}
        return {"part%d" % step: near((piece, span), types[step]) for step in steps}

    entered = near((states, channels), BF16)
    shared = dict(
        results, pre_slope=slope.pre_slope, gate_slope=slope.gate_slope, enter=ready.enter,
        leave=ready.leave, b_columns=ready.b_columns, c_columns=ready.c_columns,
        w_gate=ready.w_gate, w_in=ready.w_in,
    )
    held = call(
        back(bit, urgent),
        dict(shared, **group, received=received, entering=first.entering, leaving=first.leaving,
             entry=ready.entry, expander=ready.expander),
        dict(named(urgent), bc=near((2 * states, tokens), F32), state_in=entered, grad_in=entered),
        flops=2 * tokens * channels * depth, scratch=(graded, graded),
    )

    def added(dtype, one, two, **options):
        return call(add, dict(one=one, two=two), dict(sum=near((piece, span), dtype)), **options).sum

    far_sum = added(BF16, held.part2, swap(held.part3, TP, 1))
    distant = swap(far_sum, TP, 2)
    shared.update(
        bc=held.bc, state_in=ordered(held.state_in, far_sum), grad_in=held.grad_in
    )
    held.update(call(
        rest(others), shared, named(others),
        flops=2 * tokens * channels * depth, scratch=(graded, graded),
    ))
    own = added(F32, held.part0, distant, flops=tokens * channels * depth)
    result = call(
        total, dict(own=own, across=swap(held.part1, TP, 1)),
        dict(grad=near((piece, depth), BF16), b=near((states, tokens), F32),
             c=near((states, tokens), F32)),
    )
    return result.grad, result.b, result.c


def solution(mesh):
    in_specs = (
        P((SEQ, TP), None),
        P((SEQ, TP), None),
        P(TP, None),
        P(TP, None),
        P(TP, None),
        P(None, SEQ),
        P(None, SEQ),
        P(None, SEQ),
        P(TP),
        P(None, TP),
        P(SEQ),
    )
    out_specs = (P((SEQ, TP), None), P(None, SEQ), P(None, SEQ))
    return jax.shard_map(shards, mesh=mesh, in_specs=in_specs, out_specs=out_specs, check_vma=False)
```

```python
import jax
import jax.numpy as jnp
from jax import lax
from jax.experimental import pallas as pl
from jax.experimental.pallas import tpu as pltpu
from jax.sharding import PartitionSpec as P

HDIM = 64
LANE = 128
SLOT = 32
SEQ, TP = "seq", "tp"

F32 = jnp.float32
BF16 = jnp.bfloat16
NN = (((1,), (0,)), ((), ()))
NT = (((1,), (1,)), ((), ()))
TN = (((0,), (0,)), ((), ()))


def dot(left, right, dims=NN):
    return lax.dot_general(left, right, dims, preferred_element_type=F32)


def round_up(value, step):
    return -(-value // step) * step


def silu_slope(values):
    logistic = jax.nn.sigmoid(values)
    return logistic * (1.0 + values * (1.0 - logistic))


def iota(shape, axis):
    return lax.broadcasted_iota(jnp.int32, shape, axis)


def one_minus_exp(values):
    series = 1.0 + values * (1.0 / 7.0)
    for term in (6.0, 5.0, 4.0, 3.0, 2.0):
        series = 1.0 + values * (1.0 / term) * series
    return jnp.where(values > -0.35, -values * series, 1.0 - jnp.exp(values))


def document_counts(doc_ref):
    tokens = doc_ref.shape[1]
    rows, columns = iota((tokens, tokens), 0), iota((tokens, tokens), 1)
    first = (iota((1, tokens), 1) == 0) & (lax.axis_index(SEQ) == 0)
    mark_row = jnp.where(first, 0.0, doc_ref[...].astype(F32))
    mark_row = jnp.broadcast_to(mark_row, (tokens, tokens))
    mark_column = jnp.sum(jnp.where(rows == columns, mark_row, 0.0), axis=1, keepdims=True)
    count_column = jnp.sum(jnp.where(columns <= rows, mark_row, 0.0), axis=1, keepdims=True)
    count_row = jnp.sum(
        jnp.where(rows <= columns, jnp.broadcast_to(mark_column, (tokens, tokens)), 0.0),
        axis=0,
        keepdims=True,
    )
    return mark_column, count_column, count_row


def head_picker(heads, channels, width):
    lanes = iota((heads, width), 1)
    head = iota((heads, width), 0)
    start = lax.axis_index(TP) * channels
    low = head * HDIM - start
    owned = (lanes >= low) & (lanes < low + HDIM) & (lanes < channels)
    spare = lanes - channels
    listed = (spare == head) | (spare == head + SLOT)
    return jnp.where(owned | listed, 1.0, 0.0).astype(BF16)


def decays(log_ref, doc_ref, picker):
    tokens = log_ref.shape[1]
    mark_column, count_column, count_row = document_counts(doc_ref)
    log_rows = dot(log_ref[...], picker, TN)
    rows, columns = iota((tokens, tokens), 0), iota((tokens, tokens), 1)
    lower = jnp.where(columns <= rows, 1.0, 0.0).astype(BF16)
    cumulative = dot(lower, log_rows.astype(BF16))
    scale = jnp.where(mark_column == 1.0, 1.0, jnp.sqrt(one_minus_exp(2.0 * log_rows)))
    last_count = count_column[tokens - 1 : tokens, :]
    total = cumulative[tokens - 1 : tokens, :]
    centre = cumulative[tokens // 2 : tokens // 2 + 1, :]
    rising = jnp.exp(cumulative - centre)
    falling = jnp.exp(centre - cumulative)
    fresh = jnp.where(count_column == 0.0, 1.0, 0.0)
    inside = jnp.where(count_column == last_count, 1.0, 0.0)
    carry_in = jnp.exp(cumulative) * fresh
    carry_out = jnp.exp(total - cumulative) * inside
    factor = jnp.exp(total) * fresh[tokens - 1 : tokens, :]
    return count_column, count_row, scale, rising, falling, carry_in, carry_out, factor


def two_parts(values):
    high = values.astype(BF16)
    return high, (values - high.astype(F32)).astype(BF16)


def fine_dot(left, right, dims=NN):
    (left_high, left_low), (right_high, right_low) = two_parts(left), two_parts(right)
    small = dot(left_high, right_low, dims) + dot(left_low, right_high, dims)
    return dot(left_high, right_high, dims) + small


class Values(dict):
    __getattr__ = dict.__getitem__


class Staged:
    def __init__(self, ins, outs, through, refs):
        refs = list(refs)
        far_in = [name for name, (_, far) in ins.items() if far is True and name not in through]
        far_out = [name for name, (_, _, far) in outs.items() if far]
        self.refs = {name: refs.pop(0) for name in ins}
        made = {name: refs.pop(0) for name in outs}
        held = {name: refs.pop(0) for name in far_in}
        self.made = Values(made, **{name: refs.pop(0) for name in far_out})
        sems = refs.pop(0) if far_in or far_out or through else None
        self.rest = refs
        self.loads = {
            name: pltpu.make_async_copy(self.refs[name], held[name], sems.at[at])
            for at, name in enumerate(far_in)
        }
        self.stores = {
            name: pltpu.make_async_copy(self.made[name], made[name], sems.at[len(far_in) + at])
            for at, name in enumerate(far_out)
        }
        self.passed = [
            pltpu.make_async_copy(self.refs[name], made[name], sems.at[len(far_in + far_out) + at])
            for at, name in enumerate(through)
        ]
        self.refs.update(held)
        for copy in (*self.loads.values(), *self.passed):
            copy.start()

    def take(self, name):
        if name in self.loads:
            self.loads.pop(name).wait()
        return self.refs[name]

    def __getattr__(self, name):
        return self.take(name)

    def put(self, **values):
        for name, value in values.items():
            self.made[name][...] = value
            self.send(name)

    def send(self, name):
        if name in self.stores:
            self.stores[name].start()

    def finish(self):
        for copy in (*self.stores.values(), *self.passed):
            copy.wait()


def pin(value):
    return pltpu.with_memory_space_constraint(value, pltpu.HBM)


def near(*values):
    return (*values, False)


def far(*values):
    return (*values, True)


def staged_call(body, ins, outs, flops=0, scratch=(), through=()):
    outs = dict(outs, **{name: near(ins[name][0].shape, ins[name][0].dtype) for name in through})

    def kernel(*refs):
        staged = Staged(ins, outs, through, refs)
        body(staged, *staged.rest)
        staged.finish()

    def spec(is_far):
        return pl.BlockSpec(memory_space=pltpu.HBM if is_far else pltpu.VMEM)

    held = [
        pltpu.VMEM(value.shape, value.dtype)
        for name, (value, is_far) in ins.items()
        if is_far is True and name not in through
    ]
    held += [pltpu.VMEM(shape, dtype) for shape, dtype, is_far in outs.values() if is_far]
    copies = len(held) + len(through)
    sems = [pltpu.SemaphoreType.DMA((copies,))] if copies else []
    results = pl.pallas_call(
        kernel,
        name=body.__name__,
        out_shape=[jax.ShapeDtypeStruct(shape, dtype) for shape, dtype, _ in outs.values()],
        in_specs=[spec(is_far) for _, is_far in ins.values()],
        out_specs=[spec(is_far) for _, _, is_far in outs.values()],
        scratch_shapes=held + sems + list(scratch),
        compiler_params=pltpu.CompilerParams(vmem_limit_bytes=24 * 2**20),
        cost_estimate=pl.CostEstimate(flops=flops, bytes_accessed=2**20, transcendentals=0),
    )(*[pin(value) if is_far else value for value, is_far in ins.values()])
    return Values(zip(outs, results))


def arrived_rows(staged, name, count):
    return jnp.concatenate([staged.take(name + "%d" % step)[...] for step in range(count)], axis=0)


def in_token_order(made, values, count):
    piece = values.shape[0] // count
    for step in range(count):
        start = pl.multiple_of((lax.axis_index(TP) ^ step) * piece, piece)
        made[pl.ds(start, piece), :] = values[step * piece : (step + 1) * piece, :]
    return made[...]


def head_expander(channels, width):
    first = channels // LANE * LANE
    shape = (width - first, width)
    slot = iota(shape, 0) + (first - channels)
    lane = iota(shape, 1)
    spare = lane - channels
    head = jnp.where(slot < SLOT, slot, slot - SLOT)
    low = head * HDIM - lax.axis_index(TP) * channels
    owned = (lane >= low) & (lane < low + HDIM) & (lane < channels)
    listed = (spare == head) | (spare == head + SLOT)
    kept = (slot >= 0) & (slot < 2 * SLOT)
    return jnp.where(kept & (owned | listed), 1.0, 0.0).astype(BF16)


def encode(value, factor, channels):
    lane = iota(value.shape, 1)
    high = factor.astype(BF16).astype(F32)
    listed = jnp.where(lane < channels + SLOT, high, factor - high)
    return jnp.where(lane < channels, value, listed).astype(BF16)


def decode(message, expander):
    return dot(message[:, message.shape[1] - expander.shape[0] :], expander)


def partner_is_later(bit):
    return lax.axis_index(SEQ) % (2 * bit) < bit


def put_message(staged, state_part, grad_part, factor, channels, bit):
    message = staged.made.message
    states = state_part.shape[0]
    if message.shape[0] == states:
        part = jnp.where(partner_is_later(bit), state_part, grad_part)
        message[...] = encode(part, factor, channels)
    else:
        message[:states, :] = encode(state_part, factor, channels)
        message[states:, :] = encode(grad_part, factor, channels)


def prepare(staged):
    tokens, channels = staged.made.enter.shape
    width = staged.made.factor.shape[1]
    log_ref = staged.log
    picker = head_picker(log_ref.shape[0], channels, width)
    count_column, count_row, scale, rising, falling, carry_in, carry_out, factor = decays(
        log_ref, staged.doc, picker
    )
    staged.put(enter=carry_in[:, :channels])
    staged.put(leave=(scale * carry_out)[:, :channels])
    staged.put(rise=rising[:, :channels])
    staged.put(fall=(scale * falling)[:, :channels])
    staged.put(factor=jnp.broadcast_to(factor, staged.made.factor.shape))
    staged.put(expander=head_expander(channels, width))
    rows, columns = iota((tokens, tokens), 0), iota((tokens, tokens), 1)
    same = count_column == count_row
    causal = (rows >= columns) & same
    anticausal = (rows <= columns) & same
    b_rows, c_rows = staged.b_in[...], staged.c_in[...]
    staged.put(causal=jnp.where(causal, 1.0, 0.0))
    staged.put(crossed=jnp.where(causal, dot(c_rows, b_rows, TN), 0.0))
    staged.put(crossed_back=jnp.where(anticausal, dot(b_rows, c_rows, TN), 0.0))
    staged.put(b=b_rows)
    staged.put(c=c_rows)
    staged.put(b_columns=b_rows.astype(F32).T.astype(BF16))
    staged.put(c_columns=c_rows.astype(F32).T.astype(BF16))


def put_summary(staged, name, vectors, values):
    part = staged.made[name]
    part[...] = jnp.zeros_like(part)
    part[:, : values.shape[1]] = dot(staged.take(vectors)[...], values)


def project(staged):
    parts = lax.axis_size(TP)
    rows = arrived_rows(staged, "rows", parts)
    pre = in_token_order(staged.made.pre, dot(rows, staged.w_in[...], NT), parts)
    x_rows = (pre * jax.nn.sigmoid(pre)).astype(BF16)
    staged.put(x=x_rows)
    leaving = (x_rows.astype(F32) * staged.leave[...]).astype(BF16)
    staged.put(leaving=leaving)
    put_summary(staged, "state", "b", leaving)
    gate = in_token_order(staged.made.gate, dot(rows, staged.w_gate[...], NT), parts)
    staged.put(gated=gate * jax.nn.sigmoid(gate))


def front(staged):
    channels = staged.made.mix.shape[1]
    parts = lax.axis_size(TP)
    rows = arrived_rows(staged, "grad", parts)
    mix = in_token_order(staged.made.mix, dot(rows, staged.w_out[...], NT), parts)
    y_grads = (mix * staged.gated[...]).astype(BF16)
    staged.put(y=y_grads)
    entering = (y_grads.astype(F32) * staged.enter[...]).astype(BF16)
    staged.put(entering=entering)
    put_summary(staged, "grad", "c", entering)
    state_part, grad_part = staged.state[...], staged.made.grad[...]
    put_message(staged, state_part, grad_part, staged.factor[...], channels, 1)


def joined(mine, other, later):
    factor, state, grad = mine
    other_factor, other_state, other_grad = other
    return (
        factor * other_factor,
        jnp.where(later, other_factor * state + other_state, factor * other_state + state),
        jnp.where(later, grad + factor * other_grad, other_grad + other_factor * grad),
    )


def entered(edges, other, later):
    keep, held, back_keep, back_held = edges
    factor, state, grad = other
    return (
        jnp.where(later, keep, keep * factor),
        jnp.where(later, held, keep * state + held),
        jnp.where(later, back_keep * factor, back_keep),
        jnp.where(later, back_keep * grad + back_held, back_held),
    )


def join(channels, bit, flips):
    def join_body(staged):
        expander = staged.expander[...]
        mine = staged.factor[...], staged.state[...], staged.grad[...]
        states = mine[1].shape[0]
        others = []
        for flip in flips:
            received = staged.take("received%d" % flip)
            summaries = received[:states, :].astype(F32), received[states:, :].astype(F32)
            others.append((decode(received[:states, :], expander), *summaries))
        if "keep" in staged.refs:
            refs = staged.keep, staged.held, staged.back_keep, staged.back_held
            edges = tuple(ref[...] for ref in refs)
        else:
            one, none = jnp.ones_like(mine[0]), jnp.zeros_like(mine[0])
            edges = one, none, one, none
        later = partner_is_later(bit)
        edges, mine = entered(edges, others[0], later), joined(mine, others[0], later)
        if len(flips) == 3:
            pair, later = joined(others[1], others[2], later), partner_is_later(2 * bit)
            edges, mine = entered(edges, pair, later), joined(mine, pair, later)
        staged.put(keep=edges[0], held=edges[1], back_keep=edges[2], back_held=edges[3])
        factor, state, grad = mine
        put_message(staged, state, grad, factor, channels, bit * (len(flips) + 1))
        if "state" in staged.made:
            staged.put(state=state, grad=grad, factor=factor)

    return join_body


def slopes(staged):
    staged.put(pre_slope=silu_slope(staged.pre[...]))
    staged.put(gate_slope=staged.mix[...] * silu_slope(staged.gate[...]))


def local_vectors(staged):
    upper = staged.y[...].astype(F32) * staged.rise[...]
    lower = staged.x[...].astype(F32) * staged.fall[...]
    causal = staged.causal[...] > 0.0
    high, low = two_parts(jnp.where(causal, fine_dot(upper, lower, NT), 0.0))
    b_rows, c_rows = staged.b[...], staged.c[...]
    states = b_rows.shape[0]
    bc = staged.made.bc
    bc[:states, :] = dot(c_rows, high) + dot(c_rows, low)
    bc[states:, :] = dot(b_rows, high, NT) + dot(b_rows, low, NT)


def local_channels(staged):
    x_rows, y_grads = staged.x[...].astype(F32), staged.y[...].astype(F32)
    rise, fall, skip = staged.rise[...], staged.fall[...], staged.skip[...]
    ssm = rise * fine_dot(staged.crossed[...], x_rows * fall)
    staged.put(ssm=ssm + skip * x_rows)
    x_grad = fall * fine_dot(staged.crossed_back[...], y_grads * rise)
    staged.put(x_grad=x_grad + skip * y_grads)


def put_pieces(staged, steps, state_in, grad_in, bc, gate_ref, pre_ref):
    tp = lax.axis_index(TP)
    tokens = gate_ref.shape[0]
    piece = tokens // len(steps)
    half = pl.ds(pl.multiple_of((tp ^ steps[0]) // 2 * tokens, tokens), tokens)
    carried = dot(staged.c_columns[half, :], state_in)
    ssm_out = staged.ssm[half, :] + staged.enter[half, :] * carried
    gate_ref[...] = (ssm_out.astype(BF16).astype(F32) * staged.gate_slope[half, :]).astype(BF16)
    carried = dot(staged.b_columns[half, :], grad_in)
    x_grad = staged.x_grad[half, :] + staged.leave[half, :] * carried
    pre_ref[...] = (x_grad.astype(BF16).astype(F32) * staged.pre_slope[half, :]).astype(BF16)
    starts = [pl.multiple_of((tp ^ step) % 2 * piece, piece) for step in steps]
    gate_rows, pre_rows = (
        jnp.concatenate([ref[pl.ds(start, piece), :] for start in starts], axis=0)
        for ref in (gate_ref, pre_ref)
    )
    partial = dot(gate_rows, staged.w_gate[...]) + dot(pre_rows, staged.w_in[...])
    depth = partial.shape[1]
    for at, step in enumerate(steps):
        made = staged.made["part%d" % step]
        split = made.shape[1] - bc.shape[1]
        if split > depth:
            made[:, split - LANE : split] = jnp.zeros((piece, LANE), made.dtype)
        made[:, :depth] = partial[at * piece : (at + 1) * piece, :].astype(made.dtype)
        made[: bc.shape[0], split:] = bc.astype(made.dtype)


def back(bit, steps):
    def back_body(staged, gate_ref, pre_ref):
        entry = staged.entry[...]
        states, channels = entry.shape
        received = staged.received
        other_part = received[:, :channels].astype(F32)
        other = decode(received[...], staged.expander[...])[:, :channels]
        later = partner_is_later(bit)
        keep, held, back_keep, back_held = (
            ref[:, :channels]
            for ref in (staged.keep, staged.held, staged.back_keep, staged.back_held)
        )
        state = jnp.where(later, entry, other * entry + other_part)
        state_in = (keep * state + held).astype(BF16)
        grad_in = jnp.where(later, back_keep * other_part + back_held, back_held).astype(BF16)
        staged.put(state_in=state_in, grad_in=grad_in)
        bc = staged.made.bc
        local = staged.bc
        bc[:states, :] = local[:states, :] + dot(grad_in, staged.leaving[...], NT)
        bc[states:, :] = local[states:, :] + dot(state_in, staged.entering[...], NT)
        put_pieces(staged, steps, state_in, grad_in, bc[...], gate_ref, pre_ref)

    return back_body


def rest(steps):
    def rest_body(staged, gate_ref, pre_ref):
        state_in, grad_in = staged.state_in[...], staged.grad_in[...]
        put_pieces(staged, steps, state_in, grad_in, staged.bc[...], gate_ref, pre_ref)

    return rest_body


def add(staged):
    values = [staged.take(name)[...].astype(F32) for name in staged.refs]
    staged.put(sum=sum(values).astype(staged.made.sum.dtype))


def total(staged):
    depth = staged.made.grad.shape[1]
    states, tokens = staged.made.b.shape
    received = [staged.take(name) for name in staged.refs]
    split = received[0].shape[1] - tokens
    staged.put(grad=sum(part[:, :depth].astype(F32) for part in received).astype(BF16))
    staged.put(b=sum(part[:states, split:].astype(F32) for part in received))
    staged.put(c=sum(part[states : 2 * states, split:].astype(F32) for part in received))


def swap_masks(parts):
    masks, bit = [], parts // 2
    while bit:
        masks.append(bit)
        bit //= 2
    return masks


def shards(
    layer_input, out_grad, w_in, w_gate, w_out, b_proj, c_proj, log_decay, d_skip, entry_state,
    doc_start,
):
    owners, parts = lax.axis_size(SEQ), lax.axis_size(TP)
    assert owners > 2 and owners & (owners - 1) == 0 and parts == 4
    piece, depth = layer_input.shape
    tokens = piece * parts
    channels = w_in.shape[0]
    states = b_proj.shape[0]
    width = round_up(channels + 2 * SLOT, LANE)
    wide = near((tokens, channels), F32)
    half = near((tokens, channels), BF16)
    square = near((tokens, tokens), F32)
    row = near((states, tokens), BF16)
    column = near((tokens, states), BF16)
    summary = near((states, width), F32)

    def ordered(value, after):
        return lax.optimization_barrier((value, after))[0]

    def swap(value, axis, bit):
        size = lax.axis_size(axis)
        return lax.ppermute(value, axis, [(at, at ^ bit) for at in range(size)])

    def call(body, ins, outs, **options):
        ins = {key: near(value) if hasattr(value, "shape") else value for key, value in ins.items()}
        return staged_call(body, ins, outs, **options)

    far_ins = dict(
        doc=doc_start.reshape(1, tokens), b_in=b_proj, c_in=c_proj, w_gate=w_gate,
        w_in=w_in, w_out=w_out, rows0=layer_input, grad0=out_grad, entry=entry_state,
        skip=d_skip.reshape(1, channels),
    )
    ready = call(
        prepare, dict(log=log_decay, **{name: far(value) for name, value in far_ins.items()}),
        dict(enter=wide, leave=wide, rise=wide, fall=wide, factor=summary,
             expander=near((width - channels // LANE * LANE, width), BF16), causal=square,
             crossed=square, crossed_back=square, b=row, c=row, b_columns=column, c_columns=column),
        flops=8 * tokens * channels * tokens,
        through=("w_gate", "w_in", "w_out", "rows0", "grad0", "entry", "skip"),
    )
    grad_blocks, row_blocks = {0: out_grad}, {0: layer_input}
    masks = swap_masks(parts)
    for mask in masks:
        for blocks in (row_blocks, grad_blocks):
            for step in list(blocks):
                block = blocks[step]
                if mask != masks[0]:
                    block = ordered(block, ready.expander)
                blocks[step ^ mask] = swap(block, TP, mask)
    rows = {"rows%d" % step: block for step, block in row_blocks.items()}
    grads = {"grad%d" % step: block for step, block in grad_blocks.items()}
    rows["rows0"], grads["grad0"] = ready.rows0, ready.grad0
    both = near((2 * states, width), BF16)
    one = near((states, width), BF16)
    first = call(
        project,
        dict(rows, **dict(w_gate=ready.w_gate, w_in=ready.w_in, b=ready.b, leave=ready.leave)),
        dict(gate=wide, gated=wide, pre=wide, x=half, leaving=half, state=summary),
        flops=4 * tokens * channels * depth,
    )
    first.update(call(
        front,
        dict(grads, **dict(w_out=ready.w_out, c=ready.c, enter=ready.enter, factor=ready.factor),
             **dict(gated=first.gated, state=first.state)),
        dict(mix=wide, y=half, entering=half, grad=summary, message=both),
        flops=2 * tokens * channels * depth,
    ))
    group = dict(state=first.state, grad=first.grad, factor=ready.factor)
    message, x_rows, y_grads = first.message, first.x, first.y
    results, bit = {}, 1
    while 2 * bit < owners:
        flips = (bit, 2 * bit, 3 * bit) if 4 * bit < owners else (bit,)
        arrived = {flip: swap(message, SEQ, flip) for flip in flips}
        if bit == 1:
            slope = call(
                slopes, dict(pre=first.pre, gate=first.gate, mix=first.mix),
                dict(pre_slope=wide, gate_slope=wide), flops=tokens * channels * 32,
            )
            results.update(call(
                local_vectors,
                dict(rise=ready.rise, fall=ready.fall, causal=ready.causal, b=ready.b, c=ready.c,
                     x=x_rows, y=ordered(y_grads, slope.pre_slope)),
                dict(bc=near((2 * states, tokens), F32)), flops=8 * tokens * channels * tokens,
            ))
            arrived[flips[-1]] = ordered(arrived[flips[-1]], results["bc"])
        after = bit * (len(flips) + 1)
        last = 2 * after >= owners
        outs = dict(keep=summary, held=summary, back_keep=summary, back_held=summary,
                    message=one if last else both)
        if not last:
            outs.update(state=summary, grad=summary, factor=summary)
        group = call(
            join(channels, bit, flips),
            dict(group, expander=ready.expander,
                 **{"received%d" % flip: value for flip, value in arrived.items()}),
            outs,
        )
        message = group.pop("message")
        bit = after
    received = swap(message, SEQ, bit)
    results.update(call(
        local_channels,
        dict(rise=ready.rise, fall=ready.fall, crossed=ready.crossed,
             crossed_back=ready.crossed_back, skip=ready.skip,
             x=ordered(x_rows, group.keep), y=y_grads),
        dict(ssm=wide, x_grad=wide), flops=16 * tokens * channels * tokens,
    ))
    span = round_up(depth, LANE) + tokens
    graded = pltpu.VMEM((tokens // 2, channels), BF16)
    kept, urgent, others = (0, 2), (2, 3), (0, 1)

    def named(steps):
        types = {step: F32 if step in kept else BF16 for step in steps}
        return {"part%d" % step: near((piece, span), types[step]) for step in steps}

    entered = near((states, channels), BF16)
    shared = dict(
        results, pre_slope=slope.pre_slope, gate_slope=slope.gate_slope, enter=ready.enter,
        leave=ready.leave, b_columns=ready.b_columns, c_columns=ready.c_columns,
        w_gate=ready.w_gate, w_in=ready.w_in,
    )
    held = call(
        back(bit, urgent),
        dict(shared, **group, received=received, entering=first.entering, leaving=first.leaving,
             entry=ready.entry, expander=ready.expander),
        dict(named(urgent), bc=near((2 * states, tokens), F32), state_in=entered, grad_in=entered),
        flops=2 * tokens * channels * depth, scratch=(graded, graded),
    )

    def added(dtype, one, two, **options):
        return call(add, dict(one=one, two=two), dict(sum=near((piece, span), dtype)), **options).sum

    far_sum = added(BF16, held.part2, swap(held.part3, TP, 1))
    distant = swap(far_sum, TP, 2)
    shared.update(
        bc=held.bc, state_in=ordered(held.state_in, far_sum), grad_in=held.grad_in
    )
    held.update(call(
        rest(others), shared, named(others),
        flops=2 * tokens * channels * depth, scratch=(graded, graded),
    ))
    own = added(F32, held.part0, distant, flops=tokens * channels * depth)
    result = call(
        total, dict(own=own, across=swap(held.part1, TP, 1)),
        dict(grad=near((piece, depth), BF16), b=near((states, tokens), F32),
             c=near((states, tokens), F32)),
    )
    return result.grad, result.b, result.c


def solution(mesh):
    in_specs = (
        P((SEQ, TP), None),
        P((SEQ, TP), None),
        P(TP, None),
        P(TP, None),
        P(TP, None),
        P(None, SEQ),
        P(None, SEQ),
        P(None, SEQ),
        P(TP),
        P(None, TP),
        P(SEQ),
    )
    out_specs = (P((SEQ, TP), None), P(None, SEQ), P(None, SEQ))
    return jax.shard_map(shards, mesh=mesh, in_specs=in_specs, out_specs=out_specs, check_vma=False)
```
